32 devices in a mesh: leaf: 4 (over y, core), prow: 4 (over z), pcol: 2 (over x).
Axes of the slice: x: 2, y: 2, z: 4, core: 2. Of those that a mesh axis runs over, the one named last changes fastest.
Arguments:
- front_pivot: float32 [4, 1536, 1536], P('leaf', ('prow', 'pcol')), as said below
- front_lower: float32 [4, 6144, 1536], P('leaf', ('prow', 'pcol')), may hold values from -0.375 to 0.375
- front_rest: float32 [4, 6144, 6144], P('leaf', ('prow', 'pcol')), as said below
- parent_front: float32 [4, 8192, 4096], P('leaf', ('prow', 'pcol')), may hold values from -1.3 to 4.4, as said below
- relation: int32 [4, 6144], replicated, may hold values from 0 to 8191, as said below
Outputs:
- factor_pivot: float32 [4, 1536, 1536], P('leaf', ('prow', 'pcol'))
- factor_lower: float32 [4, 6144, 1536], P('leaf', ('prow', 'pcol'))
- parent_out: float32 [4, 8192, 4096], P('leaf', ('prow', 'pcol'))
The draws below stay inside these ranges and needn't reach their ends.
Inputs may be any that keep to these rules, and one draw needn't show every extreme that they name: Each front_pivot[g] is symmetric positive definite, with no eigenvalue under 0.3. Each front_rest[g] is symmetric, with diagonal entries between 6 and 9 and small off-diagonal entries. `parent_front`: the two column halves of one parent front together form a symmetric matrix. `relation`: for every front and every k, the entries k * 768 to (k + 1) * 768 - 1 rise strictly and lie in k * 1024 to (k + 1) * 1024 - 1, and take both ends of that range.
All inputs are finite; a program needn't handle non-finite values.
Results may differ from the reference program's by a relative error of at most 0.0029.
Values may be sent and summed in bfloat16 or wider, within the bound.
No kernel may reach another device: no remote copies, remote signals or barrier semaphores. Data moves between devices by JAX's collectives and lax.ppermute only.
A program may use at most 192 MiB of HBM per device.

```python
import jax
import jax.numpy as jnp
from jax import lax

NS = 6144
NQ = 8192
NP = 1536
FRONTS = 4
RB = 768
WB = 1024


def symmetric_front(key, pivot_order, low_diag, high_diag):
    first_key, second_key = jax.random.split(key, 2)
    shape = (FRONTS, pivot_order, pivot_order)
    noise_vals = jnp.clip(jax.random.normal(first_key, shape, jnp.float32), -6.0, 6.0)
    diagonal = jax.random.uniform(second_key, (FRONTS, pivot_order), jnp.float32, low_diag, high_diag)
    lower_part = jnp.tril(noise_vals, -1)
    symmetric = (lower_part + jnp.swapaxes(lower_part, 1, 2)) * (0.5 / pivot_order ** 0.5)
    return symmetric + diagonal[:, :, None] * jnp.eye(pivot_order, dtype=jnp.float32)[None]


def draw_front_pivot(key, part):
    inner_count = 2 * NP
    base_key = jax.random.fold_in(key, 11)
    shape = (FRONTS, NP, inner_count)
    entries = jnp.clip(jax.random.normal(base_key, shape, jnp.float32), -6.0, 6.0)
    gram = jnp.einsum('gik,gjk->gij', entries, entries, precision=lax.Precision.HIGHEST) * (3.0 / inner_count)
    symmetric = 0.5 * (gram + jnp.swapaxes(gram, 1, 2))
    return (symmetric + 0.3 * jnp.eye(NP, dtype=jnp.float32)[None]).astype(jnp.float32)


def draw_front_rest(key, part):
    return symmetric_front(jax.random.fold_in(key, 23), NS, 6.0, 9.0)


def draw_parent_front(key, part):
    half_cols = NQ // 2
    stride = max(NQ // 64, 2)
    parents = FRONTS // 2
    diag_key, near_key, far_key = jax.random.split(jax.random.fold_in(key, 53), 3)
    diag_vals = jax.random.uniform(diag_key, (parents, NQ), jnp.float32, 3.6, 4.4)
    near_vals = jax.random.uniform(near_key, (parents, NQ), jnp.float32, 0.7, 1.3)
    far_vals = jax.random.uniform(far_key, (parents, NQ), jnp.float32, 0.7, 1.3)
    rows = jnp.arange(NQ, dtype=jnp.int32)[:, None]
    halves = []
    for front_idx in range(FRONTS):
        parent = front_idx // 2
        side = front_idx % 2
        cols = side * half_cols + jnp.arange(half_cols, dtype=jnp.int32)[None, :]
        diag_row = diag_vals[parent][:, None]
        near_row = near_vals[parent][:, None]
        far_row = far_vals[parent][:, None]
        near_col = near_vals[parent][side * half_cols:(side + 1) * half_cols][None, :]
        far_col = far_vals[parent][side * half_cols:(side + 1) * half_cols][None, :]
        values = jnp.where(rows == cols, diag_row, 0.0)
        values = values - jnp.where(cols == rows + 1, near_row, 0.0)
        values = values - jnp.where(rows == cols + 1, near_col, 0.0)
        values = values - jnp.where(cols == rows + stride, far_row, 0.0)
        values = values - jnp.where(rows == cols + stride, far_col, 0.0)
        halves.append(values.astype(jnp.float32))
    return jnp.stack(halves)


def draw_relation(key, part):
    blocks = NS // RB
    block_keys = jax.random.split(jax.random.fold_in(key, 37), FRONTS * blocks)

    def one_block(sub_key):
        shuffled = jax.random.permutation(sub_key, WB - 2) + 1
        chosen_pos = jnp.sort(shuffled[:RB - 2]).astype(jnp.int32)
        return jnp.concatenate([jnp.zeros((1,), jnp.int32), chosen_pos, jnp.full((1,), WB - 1, jnp.int32)])
    chosen_all = jax.vmap(one_block)(block_keys)
    offsets = jnp.arange(FRONTS * blocks, dtype=jnp.int32) % blocks * WB
    return (chosen_all + offsets[:, None]).reshape(FRONTS, NS).astype(jnp.int32)


def level_of(stream_key, dims, cuts, least, high):
    gain, own = 1.0, jax.random.fold_in(stream_key, 6)
    for dim, parts in cuts:
        heights = jnp.exp(jax.random.uniform(jax.random.fold_in(own, dim), (parts,), jnp.float32, least / len(cuts), high / len(cuts)))
        gain = gain * jnp.repeat(heights, dims[dim] // parts).reshape([-1 if axis == dim else 1 for axis in range(len(dims))])
    return gain


def gaussian(stream_key, dims, spread, limit, shards=(), held_as=jnp.bfloat16):
    level = level_of(stream_key, dims, shards, -0.22, 0.18) if shards else 1.0
    array = jax.random.normal(stream_key, dims, jnp.float32) * spread * level
    return jnp.minimum(jnp.maximum(array, -limit), limit).astype(held_as)


def setup_inputs(seed: int = 0) -> dict:
    key_list = jax.random.split(jax.random.key(seed), 6)
    return {
        "front_pivot": draw_front_pivot(jax.random.fold_in(key_list[5], 71), 0),
        "front_lower": gaussian(key_list[1], (FRONTS, NS, NP), (NP // 6) ** -0.5, 0.375, ((0, 4), (1, 8)), jnp.float32),
        "front_rest": draw_front_rest(jax.random.fold_in(key_list[5], 71), 0),
        "parent_front": draw_parent_front(jax.random.fold_in(key_list[5], 71), 0),
        "relation": draw_relation(jax.random.fold_in(key_list[5], 71), 0),
    }


highest = lax.Precision.HIGHEST

def reference(front_pivot, front_lower, front_rest, parent_front, relation):
    pivots = []
    lowers = []
    schurs = []
    for front_idx in range(FRONTS):
        factor = jnp.linalg.cholesky(front_pivot[front_idx])
        lower_part = lax.linalg.triangular_solve(factor, front_lower[front_idx], left_side=False, lower=True, transpose_a=True)
        rounded = lax.optimization_barrier(lower_part.astype(jnp.bfloat16)).astype(jnp.float32)
        schur_block = front_rest[front_idx] - jnp.dot(rounded, rounded.T, precision=highest)
        pivots.append(factor)
        lowers.append(lower_part)
        schurs.append(schur_block)
    parent_halves = []
    for parent in range(FRONTS // 2):
        whole = jnp.concatenate([parent_front[2 * parent], parent_front[2 * parent + 1]], axis=1)
        for child_idx in (2 * parent, 2 * parent + 1):
            link_map = relation[child_idx].astype(jnp.int32)
            whole = whole.at[link_map[:, None], link_map[None, :]].add(schurs[child_idx])
        parent_halves.append(whole[:, :NQ // 2])
        parent_halves.append(whole[:, NQ // 2:])
    return (jnp.stack(pivots), jnp.stack(lowers), jnp.stack(parent_halves))
```

```python
import jax
import jax.numpy as jnp
from jax import lax
from jax.sharding import PartitionSpec as P

PW = 512
ROWS = ("prow", "pcol")
high = lax.Precision.HIGH
highest = lax.Precision.HIGHEST
bf16 = jnp.bfloat16
f32 = jnp.float32


def nt(a, b, precision=high):
    return lax.dot_general(
        a, b, (((1,), (1,)), ((), ())), precision=precision, preferred_element_type=f32
    )


def factor_blocked(matrix):
    block_order = matrix.shape[0]
    if block_order <= 128:
        factor = jnp.linalg.cholesky(matrix)
        identity = jnp.eye(block_order, dtype=jnp.float32)
        inverse = lax.linalg.triangular_solve(factor, identity, left_side=True, lower=True)
        return (factor, inverse)
    middle = block_order // 2
    top_factor, top_inverse = factor_blocked(matrix[:middle, :middle])
    lower_block = jnp.dot(matrix[middle:, :middle], top_inverse.T, precision=highest)
    reduced = matrix[middle:, middle:] - jnp.dot(lower_block, lower_block.T, precision=highest)
    bottom_factor, bottom_inverse = factor_blocked(reduced)
    mixed_inverse = -jnp.dot(
        bottom_inverse, jnp.dot(lower_block, top_inverse, precision=highest), precision=highest
    )
    upper_zeros = jnp.zeros((middle, block_order - middle), jnp.float32)
    factor = jnp.concatenate(
        [
            jnp.concatenate([top_factor, upper_zeros], axis=1),
            jnp.concatenate([lower_block, bottom_factor], axis=1),
        ],
        axis=0,
    )
    inverse = jnp.concatenate(
        [
            jnp.concatenate([top_inverse, upper_zeros], axis=1),
            jnp.concatenate([mixed_inverse, bottom_inverse], axis=1),
        ],
        axis=0,
    )
    return (factor, inverse)


def swap_cols(value, apart, first_prow=0, last_prow=None):
    rows, cols = lax.axis_size("prow"), lax.axis_size("pcol")
    last_prow = rows - 1 if last_prow is None else last_prow
    pairs = [
        (r * cols + c, r * cols + (c + apart) % cols)
        for r in range(first_prow, last_prow + 1)
        for c in range(cols)
    ]
    return lax.ppermute(value, ROWS, pairs)


def gather_rows(value, first_prow=0):
    rows, cols = lax.axis_size("prow"), lax.axis_size("pcol")
    here, across = lax.axis_index("prow"), lax.axis_index("pcol")
    ups, downs = [value], [value]
    for step in range(1, rows):
        up = [(r, r + 1) for r in range(step - 1, rows - 1) if r - step + 1 >= first_prow]
        down = [(r, r - 1) for r in range(1, rows - step + 1) if r + step - 1 >= first_prow]
        ups.append(lax.ppermute(ups[-1], "prow", up) if up else jnp.zeros_like(value))
        downs.append(lax.ppermute(downs[-1], "prow", down))
    full = jnp.zeros((rows * cols,) + value.shape, value.dtype)
    for apart in range(cols):
        if apart:
            near = [swap_cols(value, apart, first_prow)]
            up_side = near + [swap_cols(ups[s], apart, s) for s in range(1, rows)]
            down_side = near + [swap_cols(downs[s], apart, 0, rows - 1 - s) for s in range(1, rows)]
        else:
            up_side, down_side = ups, downs
        for step in range(rows):
            block = up_side[step]
            if step:
                block = jnp.where(here >= step, block, down_side[rows - step])
            place = lax.rem(here - step + rows, rows) * cols + lax.rem(across - apart + cols, cols)
            full = lax.dynamic_update_index_in_dim(full, block, place, 0)
    return full


def local(front_pivot, front_lower, front_rest, parent_front, relation):
    position = lax.axis_index(ROWS)
    pivot_rows, lower_rows = front_pivot[0], front_lower[0]
    rest_rows, parent_rows = front_rest[0], parent_front[0]
    rows_here, pivot_order = pivot_rows.shape
    block_rows, child_order = rest_rows.shape
    window, parent_half = parent_rows.shape
    places = pivot_order // rows_here
    child_half = child_order // 2
    blocks = child_half // block_rows
    rows_per_prow = rows_here * lax.axis_size("pcol")
    leaf_index = lax.axis_index("leaf")
    side_bit = leaf_index % 2
    partner = leaf_index + 1 - 2 * side_bit

    panels = pivot_order // PW
    columns = [
        gather_rows(pivot_rows[:, p * PW:(p + 1) * PW], (p * PW) // rows_per_prow).reshape(
            pivot_order, PW
        )
        for p in range(panels)
    ]

    def half_cols(values, side):
        return lax.dynamic_slice_in_dim(values, side * child_half, child_half, 1)

    kept = half_cols(rest_rows, side_bit)
    sent = half_cols(rest_rows, 1 - side_bit)
    factor_cols, lower_cols = [], []
    for p in range(panels):
        start = p * PW
        column = columns[p][start:]
        lower = lower_rows[:, start:start + PW]
        for q in range(p):
            top = factor_cols[q][start - q * PW:start - q * PW + PW]
            column = column - nt(factor_cols[q][start - q * PW:], top)
            lower = lower - nt(lower_cols[q], top)
        corner, inverse = factor_blocked(column[:PW])
        factor_cols.append(jnp.concatenate([corner, nt(column[PW:], inverse)], axis=0))
        lower = nt(lower, inverse)
        lower_cols.append(lower)
        rounded = lower.astype(bf16)
        everyone = gather_rows(rounded).reshape(child_order, PW)
        mine = lax.dynamic_slice_in_dim(everyone, side_bit * child_half, child_half, 0)
        theirs = lax.dynamic_slice_in_dim(everyone, (1 - side_bit) * child_half, child_half, 0)
        sent = sent - nt(rounded, theirs, None)
        kept = kept - nt(rounded, mine, None)
    received = lax.ppermute(
        sent.astype(bf16), "leaf", [(g, g ^ 1) for g in range(lax.axis_size("leaf"))]
    )

    window_iota = jnp.arange(window, dtype=jnp.int32)

    def tables(child):
        link_map = lax.dynamic_index_in_dim(relation, child, 0, keepdims=False)
        row_links = lax.dynamic_slice_in_dim(link_map, position * block_rows, block_rows, 0)
        col_links = lax.dynamic_slice_in_dim(link_map, side_bit * child_half, child_half, 0)
        row_table = (window_iota[:, None] + position * window == row_links[None, :]).astype(bf16)
        col_local = col_links.reshape(blocks, block_rows) - side_bit * parent_half
        col_tables = [
            (col_local[k][:, None] - k * window == window_iota[None, :]).astype(bf16)
            for k in range(blocks)
        ]
        return row_table, col_tables

    def place(values, col_tables):
        return jnp.concatenate(
            [
                jnp.dot(
                    values[:, k * block_rows:(k + 1) * block_rows],
                    col_tables[k],
                    preferred_element_type=bf16,
                )
                for k in range(blocks)
            ],
            axis=1,
        )

    own_rows, own_cols = tables(leaf_index)
    other_rows, other_cols = tables(partner)
    placed = jnp.concatenate(
        [place(kept.astype(bf16), own_cols), place(received, other_cols)], axis=0
    )
    merged = parent_rows + jnp.dot(
        jnp.concatenate([own_rows, other_rows], axis=1), placed, preferred_element_type=f32
    )

    factor_rows = jnp.concatenate(
        [
            lax.dynamic_slice_in_dim(
                jnp.concatenate([jnp.zeros((p * PW, PW), f32), factor_cols[p]], axis=0),
                position * rows_here,
                rows_here,
                0,
            )
            for p in range(panels)
        ],
        axis=1,
    )
    return (factor_rows[None], jnp.concatenate(lower_cols, axis=1)[None], merged[None])


def solution(mesh):
    split = P("leaf", ROWS, None)
    return jax.shard_map(
        local,
        mesh=mesh,
        in_specs=(split, split, split, split, P()),
        out_specs=(split, split, split),
        check_vma=False,
    )
```

```python
import math

import jax
import jax.numpy as jnp
from jax import lax
from jax.experimental import pallas as pl
from jax.experimental.pallas import tpu as pltpu
from jax.sharding import PartitionSpec as P

ROWS = ("prow", "pcol")
bf16 = jnp.bfloat16
f32 = jnp.float32
LANES = 128
SUBS = 8
VMEM_LIMIT = 56 << 20


def panel_widths(order):
    narrow = order // 6
    return (narrow, 2 * narrow, 2 * narrow, narrow)


def split(x):
    top = x.astype(bf16)
    return top, (x - top.astype(f32)).astype(bf16)


def left_parts(x):
    top, low = split(x)
    return jnp.concatenate([top, top, low], axis=1)


def right_parts(x):
    top, low = split(x)
    return jnp.concatenate([top, low, top], axis=1)


def nt(a, b):
    return lax.dot_general(a, b, (((1,), (1,)), ((), ())), preferred_element_type=f32)


def nn(a, b):
    return jnp.dot(a, b, preferred_element_type=f32)


def spread_lane(x, lane):
    return jnp.broadcast_to(x[:, lane:lane + 1], (SUBS, LANES))


def spread_sub(x, sub):
    return jnp.broadcast_to(x[sub:sub + 1, :], (SUBS, LANES))


def factor_square(square):
    lane = lax.broadcasted_iota(jnp.int32, (SUBS, LANES), 1)
    sub = lax.broadcasted_iota(jnp.int32, (SUBS, LANES), 0)
    count = LANES // SUBS
    state = [square[SUBS * r:SUBS * (r + 1), :] for r in range(count)]
    uppers, inverses = [], []
    for b in range(count):
        first = SUBS * b
        block = state[b]
        inside = (lane >= first) & (lane < first + SUBS)
        columns = [spread_lane(block, first + k) for k in range(SUBS)]
        d = [
            [spread_sub(columns[k], i) if k >= i else None for k in range(SUBS)]
            for i in range(SUBS)
        ]
        packed = jnp.where(inside, (lane - first == sub).astype(f32), block)
        corner = jnp.where(inside, block, 0.0)
        rows = [spread_sub(packed, i) for i in range(SUBS)]
        corners = [spread_sub(corner, i) for i in range(SUBS)]
        follow = b + 1 < count
        if follow:
            ahead = state[b + 1]
            beside = [spread_lane(ahead, first + k) for k in range(SUBS)]
            ahead = jnp.where(inside, 0.0, ahead)
        scales, steps = [], []
        for i in range(SUBS):
            scale = lax.rsqrt(d[i][i])
            scales.append(scale)
            rows[i] = rows[i] * scale
            corners[i] = corners[i] * scale
            step = [d[i][k] * scale if k > i else None for k in range(SUBS)]
            steps.append(step)
            if follow:
                beside[i] = beside[i] * scale
                ahead = ahead - beside[i] * rows[i]
            for k in range(i + 1, SUBS):
                for m in range(k, SUBS):
                    d[k][m] = d[k][m] - step[k] * step[m]
                rows[k] = rows[k] - step[k] * rows[i]
                corners[k] = corners[k] - step[k] * corners[i]
                if follow:
                    beside[k] = beside[k] - step[k] * beside[i]
        whole, whole_corner = rows[0], corners[0]
        for i in range(1, SUBS):
            whole = jnp.where(sub == i, rows[i], whole)
            whole_corner = jnp.where(sub == i, corners[i], whole_corner)
        inverses.append(jnp.where(lane < first + SUBS, whole, 0.0))
        upper = jnp.where(lane >= first + SUBS, whole, whole_corner)
        uppers.append(jnp.where(lane >= first + sub, upper, 0.0))
        if follow:
            state[b + 1] = ahead
        if b + 2 < count:
            back = [None] * SUBS
            for i in reversed(range(SUBS)):
                total = rows[i]
                for k in range(i + 1, SUBS):
                    total = total - steps[i][k] * back[k]
                back[i] = total * scales[i]
            for r in range(b + 2, count):
                below = state[r]
                left = [spread_lane(below, first + k) for k in range(SUBS)]
                below = jnp.where(inside, 0.0, below)
                for k in range(SUBS):
                    below = below - left[k] * back[k]
                state[r] = below
    return jnp.concatenate(uppers, axis=0), jnp.concatenate(inverses, axis=0)


def largest_tile(rows):
    return next(t for t in (256, 128, 64, 32, 16, 8) if rows % t == 0)


def panel_kernel(before, *refs):
    pivot_in, lower_in = refs[:2]
    earlier = [(refs[2 + 2 * q], refs[3 + 2 * q]) for q in range(before)]
    pivot, lower, rounded, tops = refs[2 + 2 * before:6 + 2 * before]
    crowns = refs[6 + 2 * before:]
    width = pivot.shape[1]
    count = width // LANES
    pivot_rest = pivot.shape[0] - width
    starts = [past.shape[0] - pivot.shape[0] for past, _ in earlier]
    for q in range(before):
        for t in range(count):
            crowns[q][t * LANES:(t + 1) * LANES, :] = right_parts(
                earlier[q][0][starts[q] + t * LANES:starts[q] + (t + 1) * LANES, :]
            )

    def load(source, target, pasts, offsets):
        tile = largest_tile(source.shape[0])

        @pl.loop(0, source.shape[0] // tile)
        def _(t):
            first = pl.multiple_of(t * tile, tile)
            values = source[pl.ds(first, tile), :]
            for q in range(before):
                past = pasts[q][pl.ds(pl.multiple_of(offsets[q] + first, 8), tile), :]
                values = values - nt(left_parts(past), crowns[q][...])
            target[pl.ds(first, tile), :] = values

    load(pivot_in, pivot, [past for past, _ in earlier], starts)
    load(lower_in, lower, [past for _, past in earlier], [0] * before)

    @pl.loop(0, count)
    def _(k):
        here = pl.ds(pl.multiple_of(k * LANES, LANES), LANES)
        upper, inverse = factor_square(pivot[here, here])
        pivot[here, here] = upper.T
        solver = right_parts(inverse)
        for t in range(count):
            block = slice(t * LANES, (t + 1) * LANES)

            @pl.when(t < k)
            def _():
                pivot[block, here] = jnp.zeros((LANES, LANES), f32)

            @pl.when(t > k)
            def _():
                solved = nt(left_parts(pivot[block, here]), solver)
                pivot[block, here] = solved
                tops[block, :] = right_parts(solved)

        for c in range(1, count):
            cols = slice(c * LANES, (c + 1) * LANES)

            @pl.when(c > k)
            def _():
                solved = left_parts(pivot[c * LANES:width, here])
                pivot[c * LANES:width, cols] -= nt(solved, tops[cols, :])

        def run(ref, start, rows):
            tile = largest_tile(rows)

            @pl.loop(0, rows // tile)
            def _(t):
                band = pl.ds(pl.multiple_of(start + t * tile, 8), tile)
                solved = nt(left_parts(ref[band, here]), solver)
                ref[band, here] = solved
                parts = left_parts(solved)
                for c in range(1, count):
                    cols = slice(c * LANES, (c + 1) * LANES)

                    @pl.when(c > k)
                    def _():
                        ref[band, cols] -= nt(parts, tops[cols, :])

        if pivot_rest:
            run(pivot, width, pivot_rest)
        run(lower, 0, lower.shape[0])

    tile = largest_tile(lower.shape[0])

    @pl.loop(0, lower.shape[0] // tile)
    def _(t):
        here = pl.ds(pl.multiple_of(t * tile, tile), tile)
        rounded[here, :] = lower[here, :].astype(bf16)


def factor_panel(column, lower, earlier):
    width = column.shape[1]
    before = len(earlier)
    flat = [past for pair in earlier for past in pair]
    return pl.pallas_call(
        lambda *refs: panel_kernel(before, *refs),
        out_shape=(
            jax.ShapeDtypeStruct(column.shape, f32),
            jax.ShapeDtypeStruct(lower.shape, f32),
            jax.ShapeDtypeStruct(lower.shape, bf16),
        ),
        in_specs=[pl.BlockSpec(memory_space=pltpu.VMEM)] * (2 + len(flat)),
        out_specs=[pl.BlockSpec(memory_space=pltpu.VMEM)] * 3,
        scratch_shapes=[pltpu.VMEM((width, 3 * LANES), bf16)]
        + [pltpu.VMEM((width, 3 * past.shape[1]), bf16) for past, _ in earlier],
        compiler_params=pltpu.CompilerParams(vmem_limit_bytes=VMEM_LIMIT),
        cost_estimate=pl.CostEstimate(
            flops=width * 50000000, bytes_accessed=10 * (column.size + lower.size), transcendentals=0
        ),
    )(column, lower, *flat)


def one_hot(links, window):
    places = lax.broadcasted_iota(jnp.int32, (window, links.shape[1]), 0)
    return (places == links).astype(bf16)


def rest_kernel(side, own, other, own_rows, other_rows, own_cols, other_cols, parent, out, table, placed):
    window = out.shape[0]
    rows = own.shape[0]
    for source, (values, row_links, col_links) in enumerate(
        ((own, own_rows, own_cols), (other, other_rows, other_cols))
    ):
        first = 2 * source * rows

        @pl.when(pl.program_id(0) == 0)
        def _():
            spread = one_hot(row_links[0], window)
            table[:, first:first + rows] = spread
            table[:, first + rows:first + 2 * rows] = spread

        top, low = split(values[...])
        for i in range(col_links.shape[0]):
            spread = one_hot(col_links[i, 0], window)
            block, area = slice(i * rows, (i + 1) * rows), slice(i * window, (i + 1) * window)
            placed[first:first + rows, area] = nt(top[:, block], spread).astype(bf16)
            placed[first + rows:first + 2 * rows, area] = nt(low[:, block], spread).astype(bf16)
    tile = largest_tile(window)

    @pl.loop(0, window // tile)
    def _(t):
        here = pl.ds(pl.multiple_of(t * tile, tile), tile)
        out[here, :] = parent[here, :] + nn(table[here, :], placed[...])


def add_rest(parent, rest, received, side, row_links, col_links):
    window = parent.shape[0]
    rows = rest.shape[0]
    group = LANES // math.gcd(LANES, rows)
    steps = parent.shape[1] // window // group
    links = [pl.BlockSpec((1, 1, rows), lambda w, side: (0, 0, 0))] * 2 + [
        pl.BlockSpec((group, 1, 1, rows), lambda w, side: (w, 0, 0, 0))
    ] * 2
    area = pl.BlockSpec((window, group * window), lambda w, side: (0, w))
    return pl.pallas_call(
        rest_kernel,
        out_shape=jax.ShapeDtypeStruct(parent.shape, f32),
        grid_spec=pltpu.PrefetchScalarGridSpec(
            num_scalar_prefetch=1,
            grid=(steps,),
            in_specs=[
                pl.BlockSpec((rows, group * rows), lambda w, side: (0, side[0] * steps + w)),
                pl.BlockSpec((rows, group * rows), lambda w, side: (0, w)),
            ]
            + links
            + [area],
            out_specs=area,
            scratch_shapes=[
                pltpu.VMEM((window, 4 * rows), bf16),
                pltpu.VMEM((4 * rows, group * window), bf16),
            ],
        ),
        compiler_params=pltpu.CompilerParams(vmem_limit_bytes=VMEM_LIMIT),
        cost_estimate=pl.CostEstimate(
            flops=8 * rows * parent.size + 8 * rows * rows * parent.shape[1],
            bytes_accessed=8 * parent.size + 8 * received.size,
            transcendentals=0,
        ),
    )(side, rest, received, *row_links, *col_links, parent)


def rows_kernel(own, other, own_links, other_links, out):
    window, width = out.shape[0], own.shape[1]
    for source, (values, links) in enumerate(((own, own_links), (other, other_links))):
        out[:, source * width:(source + 1) * width] = nn(
            one_hot(links[0], window), values[...]
        ).astype(bf16)


def spread_rows(own, other, row_links, window):
    return pl.pallas_call(
        rows_kernel,
        out_shape=jax.ShapeDtypeStruct((window, 2 * own.shape[1]), bf16),
        compiler_params=pltpu.CompilerParams(vmem_limit_bytes=VMEM_LIMIT),
        cost_estimate=pl.CostEstimate(
            flops=4 * window * own.size, bytes_accessed=12 * own.size, transcendentals=0
        ),
    )(own, other, *row_links)


def update_kernel(places, rows, own, other, own_links, other_links, total, out, cols):
    window, width = out.shape[0], own.shape[2]
    for source, (values, links) in enumerate(((own, own_links), (other, other_links))):
        cols[:, source * width:(source + 1) * width] = nn(
            one_hot(links[0, 0], window), values[0]
        ).astype(bf16)
    tile = largest_tile(window)

    @pl.loop(0, window // tile)
    def _(t):
        here = pl.ds(pl.multiple_of(t * tile, tile), tile)
        out[here, :] = total[here, :] - nt(rows[here, :], cols[...])


def update_windows(total, rows, own, other, places, col_links):
    window = total.shape[0]
    count, children, width = own.shape
    block = pl.BlockSpec((1, children, width), lambda i, places: (i, 0, 0))
    link = pl.BlockSpec((1, 1, 1, children), lambda i, places: (places[i], 0, 0, 0))
    area = pl.BlockSpec((window, window), lambda i, places: (0, places[i]))
    return pl.pallas_call(
        update_kernel,
        out_shape=jax.ShapeDtypeStruct(total.shape, f32),
        grid_spec=pltpu.PrefetchScalarGridSpec(
            num_scalar_prefetch=1,
            grid=(count,),
            in_specs=[
                pl.BlockSpec((window, 2 * width), lambda i, places: (0, 0)),
                block,
                block,
                link,
                link,
                area,
            ],
            out_specs=area,
            scratch_shapes=[pltpu.VMEM((window, 2 * width), bf16)],
        ),
        input_output_aliases={6: 0},
        compiler_params=pltpu.CompilerParams(vmem_limit_bytes=VMEM_LIMIT),
        cost_estimate=pl.CostEstimate(
            flops=4 * count * window * width * (window + children),
            bytes_accessed=8 * count * window * window,
            transcendentals=0,
        ),
    )(places, rows, own, other, *col_links, total)


def local(front_pivot, front_lower, front_rest, parent_front, relation):
    leaves, prows, pcols = (lax.axis_size(a) for a in ("leaf", "prow", "pcol"))
    position = lax.axis_index(ROWS)
    here, across = lax.axis_index("prow"), lax.axis_index("pcol")
    pivot_rows, lower_rows = front_pivot[0], front_lower[0]
    rest_rows, parent_rows = front_rest[0], parent_front[0]
    rows_here, pivot_order = pivot_rows.shape
    block_rows, child_order = rest_rows.shape
    window = parent_rows.shape[0]
    child_half = child_order // 2
    blocks = child_half // block_rows
    near = prows // 2
    leaf_index = lax.axis_index("leaf")
    side = leaf_index % 2
    partner = leaf_index + 1 - 2 * side

    def to_sibling(value):
        return lax.ppermute(value, "leaf", [(g, g ^ 1) for g in range(leaves)])

    def to_cols(value, apart, swap):
        pairs = [
            ((g * prows + r) * pcols + c, ((g ^ swap) * prows + r) * pcols + (c + apart) % pcols)
            for g in range(leaves)
            for r in range(prows)
            for c in range(pcols)
        ]
        return lax.ppermute(value, ("leaf",) + ROWS, pairs)

    def links_of(child):
        links = lax.dynamic_index_in_dim(relation, child, 0, keepdims=False)
        rows = lax.dynamic_slice_in_dim(links, position * block_rows, block_rows, 0)
        cols = lax.dynamic_slice_in_dim(links, side * child_half, child_half, 0)
        cols = cols.reshape(blocks, 1, 1, block_rows)
        first = side * blocks + jnp.arange(blocks, dtype=jnp.int32)
        return (
            (rows - position * window).reshape(1, 1, block_rows),
            cols - first.reshape(blocks, 1, 1, 1) * window,
        )

    own_row_links, own_col_links = links_of(leaf_index)
    other_row_links, other_col_links = links_of(partner)
    row_links = (own_row_links, other_row_links)
    col_links = (own_col_links, other_col_links)

    widths = panel_widths(pivot_order)
    starts = [sum(widths[:p]) for p in range(len(widths))]
    columns = [
        lax.all_gather(pivot_rows[:, s:s + w], ROWS, axis=0, tiled=True)
        for s, w in zip(starts, widths)
    ]

    leaving = lax.dynamic_slice_in_dim(rest_rows, (1 - side) * child_half, child_half, 1)
    total = add_rest(
        parent_rows,
        rest_rows,
        to_sibling(leaving),
        side.astype(jnp.int32).reshape(1),
        row_links,
        col_links,
    )

    done, panels = [], []
    for s, w, column in zip(starts, widths, columns):
        pivot, lower, rounded = factor_panel(column[s:], lower_rows[:, s:s + w], done)
        done.append((pivot, lower))
        other = to_sibling(rounded)
        ring = [rounded] + [
            lax.ppermute(rounded, "prow", [(r, (r + step) % prows) for r in range(prows)])
            for step in range(1, prows)
        ]
        ring = jnp.stack(ring)

        def half(which):
            first = which * near
            return jnp.stack(
                [
                    lax.dynamic_index_in_dim(
                        ring, lax.rem(here - first - i + prows, prows), 0, keepdims=False
                    )
                    for i in range(near)
                ]
            )

        kept, sent = half(side), half(1 - side)
        panels.append((rounded, other, kept, sent))

    for rounded, other, kept, sent in panels:
        rows = spread_rows(rounded, other, row_links, window)
        for apart in range(pcols):
            own = to_cols(kept, apart, 0) if apart else kept
            sibling = to_cols(sent, apart, 1)
            places = jnp.arange(near, dtype=jnp.int32) * pcols + lax.rem(
                across - apart + pcols, pcols
            ).astype(jnp.int32)
            total = update_windows(total, rows, own, sibling, places, col_links)

    factor_rows = jnp.concatenate(
        [
            lax.dynamic_slice_in_dim(
                jnp.concatenate([jnp.zeros((s, w), f32), pivot], axis=0),
                position * rows_here,
                rows_here,
                0,
            )
            for s, w, (pivot, _) in zip(starts, widths, done)
        ],
        axis=1,
    )
    lower_out = jnp.concatenate([lower for _, lower in done], axis=1)
    return (factor_rows[None], lower_out[None], total[None])


def solution(mesh):
    whole = P("leaf", ROWS, None)
    return jax.shard_map(
        local,
        mesh=mesh,
        in_specs=(whole, whole, whole, whole, P()),
        out_specs=(whole, whole, whole),
        check_vma=False,
    )
```

```python
import math

import jax
import jax.numpy as jnp
from jax import lax
from jax.experimental import pallas as pl
from jax.experimental.pallas import tpu as pltpu
from jax.sharding import PartitionSpec as P

ROWS = ("prow", "pcol")
bf16 = jnp.bfloat16
f32 = jnp.float32
LANES = 128
SUBS = 8
GROUP = 32
VMEM_LIMIT = 56 << 20


def panel_widths(order):
    narrow = order // 6
    return (narrow, 2 * narrow, 2 * narrow, narrow)


def split(x):
    top = x.astype(bf16)
    return top, (x - top.astype(f32)).astype(bf16)


def left_parts(x):
    top, low = split(x)
    return jnp.concatenate([top, top, low], axis=1)


def right_parts(x):
    top, low = split(x)
    return jnp.concatenate([top, low, top], axis=1)


def nt(a, b):
    return lax.dot_general(a, b, (((1,), (1,)), ((), ())), preferred_element_type=f32)


def nn(a, b):
    return jnp.dot(a, b, preferred_element_type=f32)


def spread_lane(x, lane):
    return jnp.broadcast_to(x[:, lane:lane + 1], (SUBS, LANES))


def spread_sub(x, sub):
    return jnp.broadcast_to(x[sub:sub + 1, :], (SUBS, LANES))


def factor_square(square):
    lane = lax.broadcasted_iota(jnp.int32, (SUBS, LANES), 1)
    sub = lax.broadcasted_iota(jnp.int32, (SUBS, LANES), 0)
    count = LANES // SUBS
    span = GROUP // SUBS
    state = [square[SUBS * r:SUBS * (r + 1), :] for r in range(count)]
    inverses = []
    for b in range(count):
        first = SUBS * b
        last = (b // span + 1) * span
        block = state[b]
        inside = (lane >= first) & (lane < first + SUBS)
        columns = [spread_lane(block, first + k) for k in range(SUBS)]
        d = [
            [spread_sub(columns[k], i) if k >= i else None for k in range(SUBS)]
            for i in range(SUBS)
        ]
        packed = jnp.where(inside, (lane - first == sub).astype(f32), block)
        rows = [spread_sub(packed, i) for i in range(SUBS)]
        follow = b + 1 < last
        if follow:
            ahead = state[b + 1]
            beside = [spread_lane(ahead, first + k) for k in range(SUBS)]
            ahead = jnp.where(inside, 0.0, ahead)
        scales, steps = [], []
        for i in range(SUBS):
            scale = lax.rsqrt(d[i][i])
            scales.append(scale)
            step = [d[i][k] * scale if k > i else None for k in range(SUBS)]
            steps.append(step)
            rows[i] = rows[i] * scale
            if follow:
                beside[i] = beside[i] * scale
                ahead = ahead - beside[i] * rows[i]
            for k in range(i + 1, SUBS):
                for m in range(k, SUBS):
                    d[k][m] = d[k][m] - step[k] * step[m]
                rows[k] = rows[k] - step[k] * rows[i]
                if follow:
                    beside[k] = beside[k] - step[k] * beside[i]
        whole = rows[0]
        for i in range(1, SUBS):
            whole = jnp.where(sub == i, rows[i], whole)
        inverses.append(whole)
        if follow:
            state[b + 1] = ahead
        if b + 2 < last:
            back = [None] * SUBS
            for i in reversed(range(SUBS)):
                total = rows[i]
                for k in range(i + 1, SUBS):
                    total = total - steps[i][k] * back[k]
                back[i] = total * scales[i]
            for r in range(b + 2, last):
                below = state[r]
                left = [spread_lane(below, first + k) for k in range(SUBS)]
                below = jnp.where(inside, 0.0, below)
                for k in range(SUBS):
                    below = below - left[k] * back[k]
                state[r] = below
        if b + 1 == last and last < count:
            start = GROUP * (b // span)
            solved = jnp.concatenate(
                [
                    jnp.where((lane >= SUBS * (g + 1)) & (lane < SUBS * last), 0.0, inverses[g])
                    for g in range(b + 1 - span, b + 1)
                ],
                axis=0,
            )
            after = jnp.concatenate(state[last:], axis=0)
            own = slice(start, start + GROUP)
            left = nt(left_parts(after[:, own]), right_parts(solved[:, own]))
            top, low = split(solved)
            change = nn(left_parts(left), jnp.concatenate([top, low, top], axis=0))
            for r in range(last, count):
                at = SUBS * (r - last)
                done = (lane >= start) & (lane < start + GROUP)
                state[r] = jnp.where(done, 0.0, state[r]) - change[at:at + SUBS, :]
    return jnp.concatenate(
        [jnp.where(lane < SUBS * (b + 1), inverses[b], 0.0) for b in range(count)], axis=0
    )


def largest_tile(rows):
    return next(t for t in (256, 128, 64, 32, 16, 8) if rows % t == 0)


def panel_kernel(first, base, bases, pcols, *refs):
    refs = list(refs)
    across, shares, refs = refs[0], refs[1:1 + pcols], refs[1 + pcols:]
    before = len(bases)
    earlier = [(refs[2 * q], refs[2 * q + 1]) for q in range(before)]
    refs = refs[2 * before:]
    lower_in, _, pivot, lower, rounded, tops = refs[:6]
    crowns = refs[6:]
    width = pivot.shape[1]
    count = width // LANES
    skip = first - base
    bottom = skip + width
    for q in range(before):
        for t in range(count):
            at = first - bases[q] + t * LANES
            crowns[q][t * LANES:(t + 1) * LANES, :] = right_parts(
                earlier[q][0][at:at + LANES, :]
            )
    share_rows = shares[0].shape[1]
    for apart in range(pcols):
        source = lax.rem(across[0] - apart + pcols, pcols)
        for r in range(shares[apart].shape[0]):
            at = pl.multiple_of((r * pcols + source) * share_rows, 8)
            pivot[pl.ds(at, share_rows), :] = shares[apart][r]
    pltpu.sync_copy(lower_in.at[:, first:first + width], lower)

    def subtract(target, pasts, offsets):
        tile = largest_tile(target.shape[0])

        @pl.loop(0, target.shape[0] // tile)
        def _(t):
            at = pl.multiple_of(t * tile, tile)
            values = target[pl.ds(at, tile), :]
            for q in range(before):
                past = pasts[q][pl.ds(pl.multiple_of(offsets[q] + at, 8), tile), :]
                values = values - nt(left_parts(past), crowns[q][...])
            target[pl.ds(at, tile), :] = values

    if before:
        subtract(pivot, [past for past, _ in earlier], [base - b for b in bases])
        subtract(lower, [past for _, past in earlier], [0] * before)
    if skip:
        pivot[0:skip, :] = jnp.zeros((skip, width), f32)

    @pl.loop(0, count)
    def _(k):
        here = pl.ds(pl.multiple_of(k * LANES, LANES), LANES)
        corner = pl.ds(pl.multiple_of(skip + k * LANES, LANES), LANES)
        square = pivot[corner, here]
        solver = right_parts(factor_square(square))
        below = lax.broadcasted_iota(jnp.int32, (LANES, LANES), 0) >= lax.broadcasted_iota(
            jnp.int32, (LANES, LANES), 1
        )
        pivot[corner, here] = jnp.where(below, nt(left_parts(square), solver), 0.0)
        for t in range(count):
            block = slice(skip + t * LANES, skip + (t + 1) * LANES)

            @pl.when(t < k)
            def _():
                pivot[block, here] = jnp.zeros((LANES, LANES), f32)

            @pl.when(t > k)
            def _():
                solved = nt(left_parts(pivot[block, here]), solver)
                pivot[block, here] = solved
                tops[t * LANES:(t + 1) * LANES, :] = right_parts(solved)

        for c in range(1, count):
            cols = slice(c * LANES, (c + 1) * LANES)

            @pl.when(c > k)
            def _():
                block = slice(skip + c * LANES, bottom)
                solved = left_parts(pivot[block, here])
                pivot[block, cols] -= nt(solved, tops[cols, :])

        def run(ref, start, rows):
            tile = largest_tile(rows)

            @pl.loop(0, rows // tile)
            def _(t):
                band = pl.ds(pl.multiple_of(start + t * tile, 8), tile)
                solved = nt(left_parts(ref[band, here]), solver)
                ref[band, here] = solved
                parts = left_parts(solved)
                for c in range(1, count):
                    cols = slice(c * LANES, (c + 1) * LANES)

                    @pl.when(c > k)
                    def _():
                        ref[band, cols] -= nt(parts, tops[cols, :])

        if pivot.shape[0] > bottom:
            run(pivot, bottom, pivot.shape[0] - bottom)
        run(lower, 0, lower.shape[0])

    tile = largest_tile(lower.shape[0])

    @pl.loop(0, lower.shape[0] // tile)
    def _(t):
        here = pl.ds(pl.multiple_of(t * tile, tile), tile)
        rounded[here, :] = lower[here, :].astype(bf16)


def factor_panel(first, across, shares, lower, earlier, after):
    prows, share_rows, width = shares[0].shape
    rows = len(shares) * prows * share_rows
    order = lower.shape[1]
    base = order - rows
    flat = [past for pair in earlier for past in pair]
    in_vmem = pl.BlockSpec(memory_space=pltpu.VMEM)
    anywhere = pl.BlockSpec(memory_space=pl.ANY)
    bases = [order - past.shape[0] for past, _ in earlier]
    return pl.pallas_call(
        lambda *refs: panel_kernel(first, base, bases, len(shares), *refs),
        out_shape=(
            jax.ShapeDtypeStruct((rows, width), f32),
            jax.ShapeDtypeStruct((lower.shape[0], width), f32),
            jax.ShapeDtypeStruct((lower.shape[0], width), bf16),
        ),
        in_specs=[pl.BlockSpec(memory_space=pltpu.SMEM)]
        + [in_vmem] * (len(shares) + len(flat))
        + [anywhere] * 2,
        out_specs=[in_vmem] * 3,
        scratch_shapes=[pltpu.VMEM((width, 3 * LANES), bf16)]
        + [pltpu.VMEM((width, 3 * past.shape[1]), bf16) for past, _ in earlier],
        compiler_params=pltpu.CompilerParams(vmem_limit_bytes=VMEM_LIMIT),
        cost_estimate=pl.CostEstimate(
            flops=width * 50000000,
            bytes_accessed=10 * width * (rows + lower.shape[0]),
            transcendentals=0,
        ),
    )(across, *shares, *flat, lower, after)


def one_hot(links, window):
    places = lax.broadcasted_iota(jnp.int32, (window, links.shape[1]), 0)
    return (places == links).astype(bf16)


def rest_kernel(first, values, row_links, col_links, parent, out, table, placed):
    window = out.shape[0]
    rows = values.shape[0]

    @pl.when(pl.program_id(0) == 0)
    def _():
        spread = one_hot(row_links[0], window)
        table[:, :rows] = spread
        table[:, rows:] = spread

    top, low = split(values[...])
    for i in range(col_links.shape[0]):
        spread = one_hot(col_links[i, 0], window)
        block, area = slice(i * rows, (i + 1) * rows), slice(i * window, (i + 1) * window)
        placed[:rows, area] = nt(top[:, block], spread).astype(bf16)
        placed[rows:, area] = nt(low[:, block], spread).astype(bf16)
    tile = largest_tile(window)

    @pl.loop(0, window // tile)
    def _(t):
        here = pl.ds(pl.multiple_of(t * tile, tile), tile)
        out[here, :] = parent[here, :] + nn(table[here, :], placed[...])


def add_rest(parent, values, half, row_links, col_links, in_place):
    window = parent.shape[0]
    rows = values.shape[0]
    group = LANES // math.gcd(LANES, rows)
    steps = parent.shape[1] // window // group
    area = pl.BlockSpec((window, group * window), lambda w, half: (0, w))
    return pl.pallas_call(
        rest_kernel,
        out_shape=jax.ShapeDtypeStruct(parent.shape, f32),
        grid_spec=pltpu.PrefetchScalarGridSpec(
            num_scalar_prefetch=1,
            grid=(steps,),
            in_specs=[
                pl.BlockSpec((rows, group * rows), lambda w, half: (0, half[0] * steps + w)),
                pl.BlockSpec((1, 1, rows), lambda w, half: (0, 0, 0)),
                pl.BlockSpec((group, 1, 1, rows), lambda w, half: (w, 0, 0, 0)),
                area,
            ],
            out_specs=area,
            scratch_shapes=[
                pltpu.VMEM((window, 2 * rows), bf16),
                pltpu.VMEM((2 * rows, group * window), bf16),
            ],
        ),
        input_output_aliases={4: 0} if in_place else {},
        compiler_params=pltpu.CompilerParams(vmem_limit_bytes=VMEM_LIMIT),
        cost_estimate=pl.CostEstimate(
            flops=4 * rows * parent.size + 4 * rows * rows * parent.shape[1],
            bytes_accessed=8 * parent.size + 4 * rows * rows * steps * group,
            transcendentals=0,
        ),
    )(half, values, row_links, col_links, parent)


def rows_kernel(own, other, own_links, other_links, out):
    window, width = out.shape[0], own.shape[1]
    for source, (values, links) in enumerate(((own, own_links), (other, other_links))):
        out[:, source * width:(source + 1) * width] = nn(
            one_hot(links[0], window), values[...]
        ).astype(bf16)


def spread_rows(own, other, row_links, window):
    return pl.pallas_call(
        rows_kernel,
        out_shape=jax.ShapeDtypeStruct((window, 2 * own.shape[1]), bf16),
        compiler_params=pltpu.CompilerParams(vmem_limit_bytes=VMEM_LIMIT),
        cost_estimate=pl.CostEstimate(
            flops=4 * window * own.size, bytes_accessed=12 * own.size, transcendentals=0
        ),
    )(own, other, *row_links)


def update_kernel(places, rows, own, other, own_links, other_links, total, out, cols):
    window, width = cols.shape[0], own.shape[2]

    @pl.when(pl.program_id(1) == 0)
    def _():
        for source, (values, links) in enumerate(((own, own_links), (other, other_links))):
            cols[:, source * width:(source + 1) * width] = nn(
                one_hot(links[0, 0], window), values[0]
            ).astype(bf16)

    out[...] = total[...] - nt(rows[...], cols[...])


def update_windows(total, rows, own, other, places, col_links):
    window = total.shape[0]
    count, children, width = own.shape
    tile = largest_tile(window)
    block = pl.BlockSpec((1, children, width), lambda i, t, places: (i, 0, 0))
    link = pl.BlockSpec((1, 1, 1, children), lambda i, t, places: (places[i], 0, 0, 0))
    area = pl.BlockSpec((tile, window), lambda i, t, places: (t, places[i]))
    return pl.pallas_call(
        update_kernel,
        out_shape=jax.ShapeDtypeStruct(total.shape, f32),
        grid_spec=pltpu.PrefetchScalarGridSpec(
            num_scalar_prefetch=1,
            grid=(count, window // tile),
            in_specs=[
                pl.BlockSpec((tile, 2 * width), lambda i, t, places: (t, 0)),
                block,
                block,
                link,
                link,
                area,
            ],
            out_specs=area,
            scratch_shapes=[pltpu.VMEM((window, 2 * width), bf16)],
        ),
        input_output_aliases={6: 0},
        compiler_params=pltpu.CompilerParams(vmem_limit_bytes=VMEM_LIMIT),
        cost_estimate=pl.CostEstimate(
            flops=4 * count * window * width * (window + children),
            bytes_accessed=8 * count * window * window,
            transcendentals=0,
        ),
    )(places, rows, own, other, *col_links, total)


def local(front_pivot, front_lower, front_rest, parent_front, relation):
    leaves, prows, pcols = (lax.axis_size(a) for a in ("leaf", "prow", "pcol"))
    position = lax.axis_index(ROWS)
    across = lax.axis_index("pcol")
    pivot_rows, lower_rows = front_pivot[0], front_lower[0]
    rest_rows, parent_rows = front_rest[0], parent_front[0]
    rows_here, pivot_order = pivot_rows.shape
    block_rows, child_order = rest_rows.shape
    window = parent_rows.shape[0]
    child_half = child_order // 2
    blocks = child_half // block_rows
    near = prows // 2
    leaf_index = lax.axis_index("leaf")
    side = leaf_index % 2
    partner = leaf_index + 1 - 2 * side

    def to_sibling(value):
        return lax.ppermute(value, "leaf", [(g, g ^ 1) for g in range(leaves)])

    def to_cols(value, apart, swap):
        pairs = [
            ((g * prows + r) * pcols + c, ((g ^ swap) * prows + r) * pcols + (c + apart) % pcols)
            for g in range(leaves)
            for r in range(prows)
            for c in range(pcols)
        ]
        return lax.ppermute(value, ("leaf",) + ROWS, pairs)

    def links_of(child):
        links = lax.dynamic_index_in_dim(relation, child, 0, keepdims=False)
        rows = lax.dynamic_slice_in_dim(links, position * block_rows, block_rows, 0)
        cols = lax.dynamic_slice_in_dim(links, side * child_half, child_half, 0)
        cols = cols.reshape(blocks, 1, 1, block_rows)
        first = side * blocks + jnp.arange(blocks, dtype=jnp.int32)
        return (
            (rows - position * window).reshape(1, 1, block_rows),
            cols - first.reshape(blocks, 1, 1, 1) * window,
        )

    own_row_links, own_col_links = links_of(leaf_index)
    other_row_links, other_col_links = links_of(partner)
    row_links = (own_row_links, other_row_links)
    col_links = (own_col_links, other_col_links)

    widths = panel_widths(pivot_order)
    starts = [sum(widths[:p]) for p in range(len(widths))]
    column_blocks = []
    for s, w in zip(starts, widths):
        mine = lax.all_gather(pivot_rows[:, s:s + w], "prow", axis=0)[s // (rows_here * pcols):]
        column_blocks.append([mine] + [to_cols(mine, apart, 0) for apart in range(1, pcols)])

    leaving = lax.dynamic_slice_in_dim(rest_rows, (1 - side) * child_half, child_half, 1)
    arrived = to_sibling(leaving)
    half = side.astype(jnp.int32).reshape(1)
    start_total = add_rest(parent_rows, rest_rows, half, own_row_links, own_col_links, False)
    total = add_rest(
        start_total, arrived, jnp.zeros((1,), jnp.int32), other_row_links, other_col_links, True
    )

    done, panels = [], []
    across_one = across.astype(jnp.int32).reshape(1)
    for p, (s, shares) in enumerate(zip(starts, column_blocks)):
        wait_for = (start_total, total)[p] if p < 2 else done[-1][0]
        pivot, lower, rounded = factor_panel(s, across_one, shares, lower_rows, done, wait_for)
        done.append((pivot, lower))
        other = to_sibling(rounded)
        line = lax.all_gather(rounded, "prow", axis=0)
        kept = lax.dynamic_slice_in_dim(line, side * near, near, 0)
        sent = lax.dynamic_slice_in_dim(line, (1 - side) * near, near, 0)
        panels.append((rounded, other, kept, sent))

    for rounded, other, kept, sent in panels:
        rows = spread_rows(rounded, other, row_links, window)
        for apart in range(pcols):
            own = to_cols(kept, apart, 0) if apart else kept
            sibling = to_cols(sent, apart, 1)
            places = jnp.arange(near, dtype=jnp.int32) * pcols + lax.rem(
                across - apart + pcols, pcols
            ).astype(jnp.int32)
            total = update_windows(total, rows, own, sibling, places, col_links)

    factor_rows = jnp.concatenate(
        [
            lax.dynamic_slice_in_dim(
                jnp.concatenate([jnp.zeros((pivot_order - pivot.shape[0], w), f32), pivot], axis=0),
                position * rows_here,
                rows_here,
                0,
            )
            for s, w, (pivot, _) in zip(starts, widths, done)
        ],
        axis=1,
    )
    lower_out = jnp.concatenate([lower for _, lower in done], axis=1)
    return (factor_rows[None], lower_out[None], total[None])


def solution(mesh):
    whole = P("leaf", ROWS, None)
    return jax.shard_map(
        local,
        mesh=mesh,
        in_specs=(whole, whole, whole, whole, P()),
        out_specs=(whole, whole, whole),
        check_vma=False,
    )
```

```python
import math

import jax
import jax.numpy as jnp
from jax import lax
from jax.experimental import pallas as pl
from jax.experimental.pallas import tpu as pltpu
from jax.sharding import PartitionSpec as P

ROWS = ("prow", "pcol")
bf16 = jnp.bfloat16
f32 = jnp.float32
LANES = 128
SUBS = 8
GROUP = 32
VMEM_LIMIT = 56 << 20


def panel_widths(order):
    narrow = order // 6
    return (narrow, 2 * narrow, 2 * narrow, narrow)


def split(x):
    top = x.astype(bf16)
    return top, (x - top.astype(f32)).astype(bf16)


def left_parts(x):
    top, low = split(x)
    return jnp.concatenate([top, top, low], axis=1)


def right_parts(x):
    top, low = split(x)
    return jnp.concatenate([top, low, top], axis=1)


def nt(a, b):
    return lax.dot_general(a, b, (((1,), (1,)), ((), ())), preferred_element_type=f32)


def nn(a, b):
    return jnp.dot(a, b, preferred_element_type=f32)


def spread_lane(x, lane):
    return jnp.broadcast_to(x[:, lane:lane + 1], (SUBS, LANES))


def spread_sub(x, sub):
    return jnp.broadcast_to(x[sub:sub + 1, :], (SUBS, LANES))


def inverse_of(x):
    guess = pl.reciprocal(x, approx=True)
    return guess * (2.0 - x * guess)


def factor_square(square):
    lane = lax.broadcasted_iota(jnp.int32, (SUBS, LANES), 1)
    sub = lax.broadcasted_iota(jnp.int32, (SUBS, LANES), 0)
    count = LANES // SUBS
    span = GROUP // SUBS
    state = [square[SUBS * r:SUBS * (r + 1), :] for r in range(count)]
    inverses = []
    for b in range(count):
        first = SUBS * b
        last = (b // span + 1) * span
        block = state[b]
        inside = (lane >= first) & (lane < first + SUBS)
        columns = [spread_lane(block, first + k) for k in range(SUBS)]
        d = [
            [spread_sub(columns[k], i) if k >= i else None for k in range(SUBS)]
            for i in range(SUBS)
        ]
        packed = jnp.where(inside, (lane - first == sub).astype(f32), block)
        rows = [spread_sub(packed, i) for i in range(SUBS)]
        follow = b + 1 < last
        if follow:
            ahead = state[b + 1]
            beside = [spread_lane(ahead, first + k) for k in range(SUBS)]
            ahead = jnp.where(inside, 0.0, ahead)
        scales, steps = [], []
        for i in range(SUBS):
            scale = inverse_of(d[i][i])
            scales.append(scale)
            step = [d[i][k] * scale if k > i else None for k in range(SUBS)]
            steps.append(step)
            for k in range(i + 1, SUBS):
                for m in range(k, SUBS):
                    d[k][m] = d[k][m] - step[k] * d[i][m]
            for k in range(i + 1, SUBS):
                rows[k] = rows[k] - step[k] * rows[i]
                if follow:
                    beside[k] = beside[k] - step[k] * beside[i]
            if follow:
                ahead = ahead - (beside[i] * scale) * rows[i]
        whole = rows[0] * lax.rsqrt(d[0][0])
        for i in range(1, SUBS):
            whole = jnp.where(sub == i, rows[i] * lax.rsqrt(d[i][i]), whole)
        inverses.append(whole)
        if follow:
            state[b + 1] = ahead
        if b + 2 < last:
            back = [None] * SUBS
            for i in reversed(range(SUBS)):
                back[i] = rows[i] * scales[i]
                for k in range(i + 1, SUBS):
                    back[i] = back[i] - steps[i][k] * back[k]
            for r in range(b + 2, last):
                below = state[r]
                left = [spread_lane(below, first + k) for k in range(SUBS)]
                below = jnp.where(inside, 0.0, below)
                for k in range(SUBS):
                    below = below - left[k] * back[k]
                state[r] = below
        if b + 1 == last and last < count:
            start = GROUP * (b // span)
            solved = jnp.concatenate(
                [
                    jnp.where((lane >= SUBS * (g + 1)) & (lane < SUBS * last), 0.0, inverses[g])
                    for g in range(b + 1 - span, b + 1)
                ],
                axis=0,
            )
            after = jnp.concatenate(state[last:], axis=0)
            own = slice(start, start + GROUP)
            left = nt(left_parts(after[:, own]), right_parts(solved[:, own]))
            top, low = split(solved)
            change = nn(left_parts(left), jnp.concatenate([top, low, top], axis=0))
            for r in range(last, count):
                at = SUBS * (r - last)
                done = (lane >= start) & (lane < start + GROUP)
                state[r] = jnp.where(done, 0.0, state[r]) - change[at:at + SUBS, :]
    return jnp.concatenate(
        [jnp.where(lane < SUBS * (b + 1), inverses[b], 0.0) for b in range(count)], axis=0
    )


def largest_tile(rows):
    return next(t for t in (256, 128, 64, 32, 16, 8) if rows % t == 0)


def panel_kernel(first, base, bases, pcols, turned, *refs):
    refs = list(refs)
    place, shares, refs = refs[0], refs[1:1 + pcols], refs[1 + pcols:]
    before = len(bases)
    earlier = [(refs[2 * q], refs[2 * q + 1]) for q in range(before)]
    refs = refs[2 * before:]
    waits = len(refs) - 4 - before
    lower_in = refs[0]
    pivot, lower, rounded, tops = refs[waits:waits + 4]
    crowns = refs[waits + 4:]
    width = pivot.shape[1]
    count = width // LANES
    skip = first - base
    bottom = skip + width
    for q in range(before):
        for t in range(count):
            at = first - bases[q] + t * LANES
            crowns[q][t * LANES:(t + 1) * LANES, :] = right_parts(
                earlier[q][0][at:at + LANES, :]
            )
    prows, share_rows = shares[0].shape[:2]
    for apart in range(pcols):
        source = lax.rem(place[1] - apart + pcols, pcols)
        for r in range(prows):
            line = lax.rem(place[0] - r + prows, prows) if turned else r
            at = pl.multiple_of((line * pcols + source) * share_rows, 8)
            pivot[pl.ds(at, share_rows), :] = shares[apart][r]
    pltpu.sync_copy(lower_in.at[:, first:first + width], lower)

    def subtract(target, pasts, offsets):
        tile = largest_tile(target.shape[0])

        @pl.loop(0, target.shape[0] // tile)
        def _(t):
            at = pl.multiple_of(t * tile, tile)
            values = target[pl.ds(at, tile), :]
            for q in range(before):
                past = pasts[q][pl.ds(pl.multiple_of(offsets[q] + at, 8), tile), :]
                values = values - nt(left_parts(past), crowns[q][...])
            target[pl.ds(at, tile), :] = values

    if before:
        subtract(pivot, [past for past, _ in earlier], [base - b for b in bases])
        subtract(lower, [past for _, past in earlier], [0] * before)
    if skip:
        pivot[0:skip, :] = jnp.zeros((skip, width), f32)

    @pl.loop(0, count)
    def _(k):
        here = pl.ds(pl.multiple_of(k * LANES, LANES), LANES)
        corner = pl.ds(pl.multiple_of(skip + k * LANES, LANES), LANES)
        square = pivot[corner, here]
        solver = right_parts(factor_square(square))
        below = lax.broadcasted_iota(jnp.int32, (LANES, LANES), 0) >= lax.broadcasted_iota(
            jnp.int32, (LANES, LANES), 1
        )
        pivot[corner, here] = jnp.where(below, nt(left_parts(square), solver), 0.0)
        for t in range(count):
            block = slice(skip + t * LANES, skip + (t + 1) * LANES)

            @pl.when(t < k)
            def _():
                pivot[block, here] = jnp.zeros((LANES, LANES), f32)

            @pl.when(t > k)
            def _():
                solved = nt(left_parts(pivot[block, here]), solver)
                pivot[block, here] = solved
                tops[t * LANES:(t + 1) * LANES, :] = right_parts(solved)

        for c in range(1, count):
            cols = slice(c * LANES, (c + 1) * LANES)

            @pl.when(c > k)
            def _():
                block = slice(skip + c * LANES, bottom)
                solved = left_parts(pivot[block, here])
                pivot[block, cols] -= nt(solved, tops[cols, :])

        def run(ref, start, rows):
            tile = largest_tile(rows)

            @pl.loop(0, rows // tile)
            def _(t):
                band = pl.ds(pl.multiple_of(start + t * tile, 8), tile)
                solved = nt(left_parts(ref[band, here]), solver)
                ref[band, here] = solved
                parts = left_parts(solved)
                for c in range(1, count):
                    cols = slice(c * LANES, (c + 1) * LANES)

                    @pl.when(c > k)
                    def _():
                        ref[band, cols] -= nt(parts, tops[cols, :])

        if pivot.shape[0] > bottom:
            run(pivot, bottom, pivot.shape[0] - bottom)
        run(lower, 0, lower.shape[0])

    tile = largest_tile(lower.shape[0])

    @pl.loop(0, lower.shape[0] // tile)
    def _(t):
        here = pl.ds(pl.multiple_of(t * tile, tile), tile)
        rounded[here, :] = lower[here, :].astype(bf16)


def factor_panel(first, place, shares, turned, lower, earlier, after):
    prows, share_rows, width = shares[0].shape
    rows = len(shares) * prows * share_rows
    order = lower.shape[1]
    base = order - rows
    flat = [past for pair in earlier for past in pair]
    in_vmem = pl.BlockSpec(memory_space=pltpu.VMEM)
    anywhere = pl.BlockSpec(memory_space=pl.ANY)
    bases = [order - past.shape[0] for past, _ in earlier]
    return pl.pallas_call(
        lambda *refs: panel_kernel(first, base, bases, len(shares), turned, *refs),
        out_shape=(
            jax.ShapeDtypeStruct((rows, width), f32),
            jax.ShapeDtypeStruct((lower.shape[0], width), f32),
            jax.ShapeDtypeStruct((lower.shape[0], width), bf16),
        ),
        in_specs=[pl.BlockSpec(memory_space=pltpu.SMEM)]
        + [in_vmem] * (len(shares) + len(flat))
        + [anywhere] * (1 + len(after)),
        out_specs=[in_vmem] * 3,
        scratch_shapes=[pltpu.VMEM((width, 3 * LANES), bf16)]
        + [pltpu.VMEM((width, 3 * past.shape[1]), bf16) for past, _ in earlier],
        compiler_params=pltpu.CompilerParams(vmem_limit_bytes=VMEM_LIMIT),
        cost_estimate=pl.CostEstimate(
            flops=width * 50000000,
            bytes_accessed=10 * width * (rows + lower.shape[0]),
            transcendentals=0,
        ),
    )(place, *shares, *flat, lower, *after)


def one_hot(links, window):
    places = lax.broadcasted_iota(jnp.int32, (window, links.shape[1]), 0)
    return (places == links).astype(bf16)


def rest_kernel(first, values, *refs):
    if len(refs) == 8:
        crossing, row_links, col_links, parent, out, leaving, table, placed = refs
        leaving[...] = crossing[...]
    else:
        row_links, col_links, parent, out, table, placed = refs
    window = out.shape[0]
    rows = values.shape[0]

    @pl.when(pl.program_id(0) == 0)
    def _():
        spread = one_hot(row_links[0], window)
        table[:, :rows] = spread
        table[:, rows:] = spread

    top, low = split(values[...])
    for i in range(col_links.shape[0]):
        spread = one_hot(col_links[i, 0], window)
        block, area = slice(i * rows, (i + 1) * rows), slice(i * window, (i + 1) * window)
        placed[:rows, area] = nt(top[:, block], spread).astype(bf16)
        placed[rows:, area] = nt(low[:, block], spread).astype(bf16)
    tile = largest_tile(out.shape[1])

    @pl.loop(0, out.shape[1] // tile)
    def _(t):
        here = pl.ds(pl.multiple_of(t * tile, tile), tile)
        out[:, here] = parent[:, here] + nn(table[...], placed[:, here])


def add_rest(parent, values, half, row_links, col_links, whole):
    window = parent.shape[0]
    rows = values.shape[0]
    group = LANES // math.gcd(LANES, rows)
    steps = parent.shape[1] // window // group
    area = pl.BlockSpec((window, group * window), lambda w, half: (0, w))
    block = (rows, group * rows)
    total = jax.ShapeDtypeStruct(parent.shape, f32)
    crossing = [pl.BlockSpec(block, lambda w, half: (0, (1 - half[0]) * steps + w))]
    leaving = pl.BlockSpec(block, lambda w, half: (0, w))
    return pl.pallas_call(
        rest_kernel,
        out_shape=(total, jax.ShapeDtypeStruct((rows, values.shape[1] // 2), f32)) if whole else total,
        grid_spec=pltpu.PrefetchScalarGridSpec(
            num_scalar_prefetch=1,
            grid=(steps,),
            in_specs=[pl.BlockSpec(block, lambda w, half: (0, half[0] * steps + w))]
            + (crossing if whole else [])
            + [
                pl.BlockSpec((1, 1, rows), lambda w, half: (0, 0, 0)),
                pl.BlockSpec((group, 1, 1, rows), lambda w, half: (w, 0, 0, 0)),
                area,
            ],
            out_specs=(area, leaving) if whole else area,
            scratch_shapes=[
                pltpu.VMEM((window, 2 * rows), bf16),
                pltpu.VMEM((2 * rows, group * window), bf16),
            ],
        ),
        input_output_aliases={} if whole else {4: 0},
        compiler_params=pltpu.CompilerParams(vmem_limit_bytes=VMEM_LIMIT),
        cost_estimate=pl.CostEstimate(
            flops=4 * rows * parent.size + 4 * rows * rows * parent.shape[1],
            bytes_accessed=8 * parent.size + 4 * rows * rows * steps * group,
            transcendentals=0,
        ),
    )(half, *([values] * (2 if whole else 1)), row_links, col_links, parent)


def rows_kernel(own, other, own_links, other_links, out):
    window, width = out.shape[0], own.shape[1]
    for source, (values, links) in enumerate(((own, own_links), (other, other_links))):
        out[:, source * width:(source + 1) * width] = nn(
            one_hot(links[0], window), values[...]
        ).astype(bf16)


def spread_rows(own, other, row_links, window):
    return pl.pallas_call(
        rows_kernel,
        out_shape=jax.ShapeDtypeStruct((window, 2 * own.shape[1]), bf16),
        compiler_params=pltpu.CompilerParams(vmem_limit_bytes=VMEM_LIMIT),
        cost_estimate=pl.CostEstimate(
            flops=4 * window * own.size, bytes_accessed=12 * own.size, transcendentals=0
        ),
    )(own, other, *row_links)


def update_kernel(places, rows, own, other, own_links, other_links, total, out, cols):
    window, width = cols.shape[0], own.shape[2]

    @pl.when(pl.program_id(1) == 0)
    def _():
        for source, (values, links) in enumerate(((own, own_links), (other, other_links))):
            cols[:, source * width:(source + 1) * width] = nn(
                one_hot(links[0, 0], window), values[0]
            ).astype(bf16)

    tile = out.shape[1]
    here = pl.ds(pl.multiple_of(pl.program_id(1) * tile, tile), tile)
    out[...] = total[...] - nt(rows[...], cols[here, :])


def update_windows(total, rows, own, other, places, col_links):
    window = total.shape[0]
    count, children, width = own.shape
    tile = largest_tile(window)
    block = pl.BlockSpec((1, children, width), lambda i, t, places: (i, 0, 0))
    link = pl.BlockSpec((1, 1, 1, children), lambda i, t, places: (places[i], 0, 0, 0))
    area = pl.BlockSpec(
        (window, tile), lambda i, t, places: (0, places[i] * (window // tile) + t)
    )
    return pl.pallas_call(
        update_kernel,
        out_shape=jax.ShapeDtypeStruct(total.shape, f32),
        grid_spec=pltpu.PrefetchScalarGridSpec(
            num_scalar_prefetch=1,
            grid=(count, window // tile),
            in_specs=[
                pl.BlockSpec((window, 2 * width), lambda i, t, places: (0, 0)),
                block,
                block,
                link,
                link,
                area,
            ],
            out_specs=area,
            scratch_shapes=[pltpu.VMEM((window, 2 * width), bf16)],
        ),
        input_output_aliases={6: 0},
        compiler_params=pltpu.CompilerParams(vmem_limit_bytes=VMEM_LIMIT),
        cost_estimate=pl.CostEstimate(
            flops=4 * count * window * width * (window + children),
            bytes_accessed=8 * count * window * window,
            transcendentals=0,
        ),
    )(places, rows, own, other, *col_links, total)


def local(front_pivot, front_lower, front_rest, parent_front, relation):
    leaves, prows, pcols = (lax.axis_size(a) for a in ("leaf", "prow", "pcol"))
    position = lax.axis_index(ROWS)
    across = lax.axis_index("pcol")
    pivot_rows, lower_rows = front_pivot[0], front_lower[0]
    rest_rows, parent_rows = front_rest[0], parent_front[0]
    rows_here, pivot_order = pivot_rows.shape
    block_rows, child_order = rest_rows.shape
    window = parent_rows.shape[0]
    child_half = child_order // 2
    blocks = child_half // block_rows
    near = prows // 2
    leaf_index = lax.axis_index("leaf")
    side = leaf_index % 2
    partner = leaf_index + 1 - 2 * side

    def to_sibling(value):
        return lax.ppermute(value, "leaf", [(g, g ^ 1) for g in range(leaves)])

    def to_cols(value, apart, swap):
        pairs = [
            ((g * prows + r) * pcols + c, ((g ^ swap) * prows + r) * pcols + (c + apart) % pcols)
            for g in range(leaves)
            for r in range(prows)
            for c in range(pcols)
        ]
        return lax.ppermute(value, ("leaf",) + ROWS, pairs)

    def links_of(child):
        links = lax.dynamic_index_in_dim(relation, child, 0, keepdims=False)
        rows = lax.dynamic_slice_in_dim(links, position * block_rows, block_rows, 0)
        cols = lax.dynamic_slice_in_dim(links, side * child_half, child_half, 0)
        cols = cols.reshape(blocks, 1, 1, block_rows)
        first = side * blocks + jnp.arange(blocks, dtype=jnp.int32)
        return (
            (rows - position * window).reshape(1, 1, block_rows),
            cols - first.reshape(blocks, 1, 1, 1) * window,
        )

    own_row_links, own_col_links = links_of(leaf_index)
    other_row_links, other_col_links = links_of(partner)
    row_links = (own_row_links, other_row_links)
    col_links = (own_col_links, other_col_links)

    widths = panel_widths(pivot_order)
    starts = [sum(widths[:p]) for p in range(len(widths))]
    def along(value, step):
        return lax.ppermute(value, "prow", [(r, (r + step) % prows) for r in range(prows)])

    column_blocks = []
    for p, (s, w) in enumerate(zip(starts, widths)):
        mine = pivot_rows[:, s:s + w]
        if p == 0:
            mine = jnp.stack([mine] + [along(mine, step) for step in range(1, prows)])
        else:
            mine = lax.all_gather(mine, "prow", axis=0)[s // (rows_here * pcols):]
        column_blocks.append([mine] + [to_cols(mine, apart, 0) for apart in range(1, pcols)])

    half = side.astype(jnp.int32).reshape(1)
    start_total, leaving = add_rest(
        parent_rows, rest_rows, half, own_row_links, own_col_links, True
    )
    total = add_rest(
        start_total,
        to_sibling(leaving),
        jnp.zeros((1,), jnp.int32),
        other_row_links,
        other_col_links,
        False,
    )

    done, panels = [], []
    place = jnp.stack([lax.axis_index("prow"), across]).astype(jnp.int32)
    for p, (s, shares) in enumerate(zip(starts, column_blocks)):
        waits = [(start_total,), (total,)][p] if p < 2 else panels[p - 2][2:]
        if 0 < p < len(starts) - 1:
            waits = waits + (column_blocks[p + 1][0],)
        pivot, lower, rounded = factor_panel(s, place, shares, p == 0, lower_rows, done, waits)
        done.append((pivot, lower))
        other = to_sibling(rounded)
        line = lax.all_gather(rounded, "prow", axis=0)
        kept = lax.dynamic_slice_in_dim(line, side * near, near, 0)
        sent = lax.dynamic_slice_in_dim(line, (1 - side) * near, near, 0)
        panels.append((rounded, other, kept, sent))

    for rounded, other, kept, sent in panels:
        rows = spread_rows(rounded, other, row_links, window)
        for apart in range(pcols):
            own = to_cols(kept, apart, 0) if apart else kept
            sibling = to_cols(sent, apart, 1)
            places = jnp.arange(near, dtype=jnp.int32) * pcols + lax.rem(
                across - apart + pcols, pcols
            ).astype(jnp.int32)
            total = update_windows(total, rows, own, sibling, places, col_links)

    factor_rows = jnp.concatenate(
        [
            lax.dynamic_slice_in_dim(
                jnp.concatenate([jnp.zeros((pivot_order - pivot.shape[0], w), f32), pivot], axis=0),
                position * rows_here,
                rows_here,
                0,
            )
            for s, w, (pivot, _) in zip(starts, widths, done)
        ],
        axis=1,
    )
    lower_out = jnp.concatenate([lower for _, lower in done], axis=1)
    return (factor_rows[None], lower_out[None], total[None])


def solution(mesh):
    whole = P("leaf", ROWS, None)
    return jax.shard_map(
        local,
        mesh=mesh,
        in_specs=(whole, whole, whole, whole, P()),
        out_specs=(whole, whole, whole),
        check_vma=False,
    )
```

```python
import math

import jax
import jax.numpy as jnp
from jax import lax
from jax.experimental import pallas as pl
from jax.experimental.pallas import tpu as pltpu
from jax.sharding import PartitionSpec as P

ROWS = ("prow", "pcol")
bf16 = jnp.bfloat16
f32 = jnp.float32
LANES = 128
SUBS = 8
GROUP = 32
TALL = 768
VMEM_LIMIT = 56 << 20


def panel_widths(order):
    narrow = order // 6
    return (narrow, 2 * narrow, 2 * narrow, narrow)


def split(x):
    top = x.astype(bf16)
    return top, (x - top.astype(f32)).astype(bf16)


def left_parts(x):
    top, low = split(x)
    return jnp.concatenate([top, top, low], axis=1)


def right_parts(x):
    top, low = split(x)
    return jnp.concatenate([top, low, top], axis=1)


def nt(a, b):
    return lax.dot_general(a, b, (((1,), (1,)), ((), ())), preferred_element_type=f32)


def nn(a, b):
    return jnp.dot(a, b, preferred_element_type=f32)


def spread_lane(x, lane):
    return jnp.broadcast_to(x[:, lane:lane + 1], (SUBS, LANES))


def spread_sub(x, sub):
    return jnp.broadcast_to(x[sub:sub + 1, :], (SUBS, LANES))


def factor_square(square):
    lane = lax.broadcasted_iota(jnp.int32, (SUBS, LANES), 1)
    sub = lax.broadcasted_iota(jnp.int32, (SUBS, LANES), 0)
    count = LANES // SUBS
    span = GROUP // SUBS
    state = [square[SUBS * r:SUBS * (r + 1), :] for r in range(count)]
    inverses = []
    for b in range(count):
        first = SUBS * b
        last = (b // span + 1) * span
        block = state[b]
        inside = (lane >= first) & (lane < first + SUBS)
        columns = [spread_lane(block, first + k) for k in range(SUBS)]
        d = [
            [spread_sub(columns[k], i) if k >= i else None for k in range(SUBS)]
            for i in range(SUBS)
        ]
        packed = jnp.where(inside, (lane - first == sub).astype(f32), block)
        rows = [spread_sub(packed, i) for i in range(SUBS)]
        follow = b + 1 < last
        if follow:
            ahead = state[b + 1]
            beside = [spread_lane(ahead, first + k) for k in range(SUBS)]
            ahead = jnp.where(inside, 0.0, ahead)
        scales, steps = [], []
        for i in range(SUBS):
            scale = lax.rsqrt(d[i][i])
            scales.append(scale)
            step = [d[i][k] * scale if k > i else None for k in range(SUBS)]
            steps.append(step)
            rows[i] = rows[i] * scale
            for k in range(i + 1, SUBS):
                for m in range(k, SUBS):
                    d[k][m] = d[k][m] - step[k] * step[m]
            for k in range(i + 1, SUBS):
                rows[k] = rows[k] - step[k] * rows[i]
            if follow:
                beside[i] = beside[i] * scale
                ahead = ahead - beside[i] * rows[i]
                for k in range(i + 1, SUBS):
                    beside[k] = beside[k] - step[k] * beside[i]
        whole = rows[0]
        for i in range(1, SUBS):
            whole = jnp.where(sub == i, rows[i], whole)
        inverses.append(whole)
        if follow:
            state[b + 1] = ahead
        if b + 2 < last:
            back = [None] * SUBS
            for i in reversed(range(SUBS)):
                total = rows[i]
                for k in range(i + 1, SUBS):
                    total = total - steps[i][k] * back[k]
                back[i] = total * scales[i]
            for r in range(b + 2, last):
                below = state[r]
                left = [spread_lane(below, first + k) for k in range(SUBS)]
                below = jnp.where(inside, 0.0, below)
                for k in range(SUBS):
                    below = below - left[k] * back[k]
                state[r] = below
        if b + 1 == last and last < count:
            start = GROUP * (b // span)
            solved = jnp.concatenate(
                [
                    jnp.where((lane >= SUBS * (g + 1)) & (lane < SUBS * last), 0.0, inverses[g])
                    for g in range(b + 1 - span, b + 1)
                ],
                axis=0,
            )
            after = jnp.concatenate(state[last:], axis=0)
            own = slice(start, start + GROUP)
            left = nt(left_parts(after[:, own]), right_parts(solved[:, own]))
            top, low = split(solved)
            change = nn(left_parts(left), jnp.concatenate([top, low, top], axis=0))
            for r in range(last, count):
                at = SUBS * (r - last)
                done = (lane >= start) & (lane < start + GROUP)
                state[r] = jnp.where(done, 0.0, state[r]) - change[at:at + SUBS, :]
    return jnp.concatenate(
        [jnp.where(lane < SUBS * (b + 1), inverses[b], 0.0) for b in range(count)], axis=0
    )


def largest_tile(rows):
    return next(t for t in (256, 128, 64, 32, 16, 8) if rows % t == 0)


def tall_tile(rows):
    return next(rows // n for n in range(1, rows) if rows % n == 0 and rows // n <= TALL)


def panel_kernel(first, base, bases, pcols, turned, corner_at, *refs):
    refs = list(refs)
    place, shares, refs = refs[0], refs[1:1 + pcols], refs[1 + pcols:]
    before = len(bases)
    earlier = [(refs[2 * q], refs[2 * q + 1]) for q in range(before)]
    refs = refs[2 * before:]
    waits = len(refs) - 5 - before
    lower_in = refs[0]
    pivot, lower, rounded, side, tops = refs[waits:waits + 5]
    crowns = refs[waits + 5:]
    side[0] = place[2]
    width = pivot.shape[1]
    count = width // LANES
    skip = first - base
    bottom = skip + width
    for q in range(before):
        for t in range(count):
            at = first - bases[q] + t * LANES
            crowns[q][t * LANES:(t + 1) * LANES, :] = right_parts(
                earlier[q][0][at:at + LANES, :]
            )
    low, left = corner_at
    prows, share_rows = shares[0].shape[:2]
    for apart in range(pcols):
        source = lax.rem(place[1] - apart + pcols, pcols)
        for r in range(prows - low):
            line = lax.rem(place[0] - r + prows, prows) if turned else r
            at = pl.multiple_of((line * pcols + source) * share_rows, 8)
            pivot[pl.ds(at, share_rows), :] = shares[apart][low + r, :, left:left + width]
    pltpu.sync_copy(lower_in.at[:, first:first + width], lower)

    def subtract(target, pasts, offsets):
        tile = tall_tile(target.shape[0])

        @pl.loop(0, target.shape[0] // tile)
        def _(t):
            at = pl.multiple_of(t * tile, tile)
            values = target[pl.ds(at, tile), :]
            for q in range(before):
                past = pasts[q][pl.ds(pl.multiple_of(offsets[q] + at, 8), tile), :]
                values = values - nt(left_parts(past), crowns[q][...])
            target[pl.ds(at, tile), :] = values

    if before:
        subtract(pivot, [past for past, _ in earlier], [base - b for b in bases])
        subtract(lower, [past for _, past in earlier], [0] * before)
    if skip:
        pivot[0:skip, :] = jnp.zeros((skip, width), f32)

    row = lax.broadcasted_iota(jnp.int32, (width, LANES), 0)
    lane = lax.broadcasted_iota(jnp.int32, (width, LANES), 1)

    @pl.loop(0, count)
    def _(k):
        here = pl.ds(pl.multiple_of(k * LANES, LANES), LANES)
        corner = pl.ds(pl.multiple_of(skip + k * LANES, LANES), LANES)
        solver = right_parts(factor_square(pivot[corner, here]))
        solved = nt(left_parts(pivot[skip:bottom, here]), solver)
        solved = jnp.where(row - k * LANES >= lane, solved, 0.0)
        pivot[skip:bottom, here] = solved
        solved = jnp.where(row >= (k + 1) * LANES, solved, 0.0)
        tops[...] = right_parts(solved)
        if count > 1:
            pivot[skip:bottom, LANES:] -= nt(left_parts(solved), tops[LANES:, :])

        def run(ref, start, rows):
            tile = tall_tile(rows)

            @pl.loop(0, rows // tile)
            def _(t):
                band = pl.ds(pl.multiple_of(start + t * tile, 8), tile)
                solved = nt(left_parts(ref[band, here]), solver)
                ref[band, here] = solved
                if count > 1:
                    ref[band, LANES:] -= nt(left_parts(solved), tops[LANES:, :])

        if pivot.shape[0] > bottom:
            run(pivot, bottom, pivot.shape[0] - bottom)
        run(lower, 0, lower.shape[0])

    tile = largest_tile(lower.shape[0])

    @pl.loop(0, lower.shape[0] // tile)
    def _(t):
        here = pl.ds(pl.multiple_of(t * tile, tile), tile)
        rounded[here, :] = lower[here, :].astype(bf16)


def factor_panel(first, width, place, shares, turned, corner_at, lower, earlier, after):
    prows, share_rows, _ = shares[0].shape
    rows = len(shares) * (prows - corner_at[0]) * share_rows
    order = lower.shape[1]
    base = order - rows
    flat = [past for pair in earlier for past in pair]
    in_vmem = pl.BlockSpec(memory_space=pltpu.VMEM)
    anywhere = pl.BlockSpec(memory_space=pl.ANY)
    bases = [order - past.shape[0] for past, _ in earlier]
    return pl.pallas_call(
        lambda *refs: panel_kernel(first, base, bases, len(shares), turned, corner_at, *refs),
        out_shape=(
            jax.ShapeDtypeStruct((rows, width), f32),
            jax.ShapeDtypeStruct((lower.shape[0], width), f32),
            jax.ShapeDtypeStruct((lower.shape[0], width), bf16),
            jax.ShapeDtypeStruct((1,), jnp.int32),
        ),
        in_specs=[pl.BlockSpec(memory_space=pltpu.SMEM)]
        + [in_vmem] * (len(shares) + len(flat))
        + [anywhere] * (1 + len(after)),
        out_specs=[in_vmem] * 3 + [pl.BlockSpec(memory_space=pltpu.SMEM)],
        scratch_shapes=[pltpu.VMEM((width, 3 * LANES), bf16)]
        + [pltpu.VMEM((width, 3 * past.shape[1]), bf16) for past, _ in earlier],
        compiler_params=pltpu.CompilerParams(vmem_limit_bytes=VMEM_LIMIT),
        cost_estimate=pl.CostEstimate(
            flops=width * 50000000,
            bytes_accessed=10 * width * (rows + lower.shape[0]),
            transcendentals=0,
        ),
    )(place, *shares, *flat, lower, *after)


def one_hot(links, window):
    places = lax.broadcasted_iota(jnp.int32, (window, links.shape[1]), 0)
    return (places == links).astype(bf16)


def rest_kernel(half, values, *refs):
    if len(refs) == 9:
        crossing, row_links, col_links, parent, _, out, leaving, table, placed = refs
        leaving[...] = crossing[...]
    else:
        row_links, col_links, parent, out, table, placed = refs
    window = out.shape[0]
    rows = values.shape[0]

    @pl.when(pl.program_id(0) == 0)
    def _():
        spread = one_hot(row_links[0], window)
        table[:, :rows] = spread
        table[:, rows:] = spread

    tile = largest_tile(out.shape[1])
    count = col_links.shape[0]
    step = pl.program_id(0)
    mine = (half[1] >= step * count) & (half[1] < (step + 1) * count)

    def spread_of(part, at, depth):
        for i in range(count):
            spread = one_hot(col_links[i, 0], window)
            block, area = slice(i * rows, (i + 1) * rows), slice(i * window, (i + 1) * window)
            placed[at:at + rows, area] = nt(part[:, block], spread).astype(bf16)
        if depth:

            @pl.loop(0, out.shape[1] // tile)
            def _(t):
                here = pl.ds(pl.multiple_of(t * tile, tile), tile)
                out[:, here] = parent[:, here] + nn(table[:, :depth], placed[:depth, here])

    @pl.when(mine)
    def _():
        top, low = split(values[...])
        spread_of(top, 0, 0)
        spread_of(low, rows, 2 * rows)

    @pl.when(jnp.logical_not(mine))
    def _():
        spread_of(values[...].astype(bf16), 0, rows)


def add_rest(parent, values, half, row_links, col_links, after):
    whole = after is not None
    window = parent.shape[0]
    rows = values.shape[0]
    group = LANES // math.gcd(LANES, rows)
    steps = parent.shape[1] // window // group
    area = pl.BlockSpec((window, group * window), lambda w, half: (0, w))
    block = (rows, group * rows)
    total = jax.ShapeDtypeStruct(parent.shape, f32)
    crossing = [pl.BlockSpec(block, lambda w, half: (0, (1 - half[0]) * steps + w))]
    leaving = pl.BlockSpec(block, lambda w, half: (0, w))
    return pl.pallas_call(
        rest_kernel,
        out_shape=(total, jax.ShapeDtypeStruct((rows, values.shape[1] // 2), f32)) if whole else total,
        grid_spec=pltpu.PrefetchScalarGridSpec(
            num_scalar_prefetch=1,
            grid=(steps,),
            in_specs=[pl.BlockSpec(block, lambda w, half: (0, half[0] * steps + w))]
            + (crossing if whole else [])
            + [
                pl.BlockSpec((1, 1, rows), lambda w, half: (0, 0, 0)),
                pl.BlockSpec((group, 1, 1, rows), lambda w, half: (w, 0, 0, 0)),
                area,
            ]
            + ([pl.BlockSpec(memory_space=pl.ANY)] if whole else []),
            out_specs=(area, leaving) if whole else area,
            scratch_shapes=[
                pltpu.VMEM((window, 2 * rows), bf16),
                pltpu.VMEM((2 * rows, group * window), bf16),
            ],
        ),
        input_output_aliases={} if whole else {4: 0},
        compiler_params=pltpu.CompilerParams(vmem_limit_bytes=VMEM_LIMIT),
        cost_estimate=pl.CostEstimate(
            flops=4 * rows * parent.size + 4 * rows * rows * parent.shape[1],
            bytes_accessed=8 * parent.size + 4 * rows * rows * steps * group,
            transcendentals=0,
        ),
    )(
        half,
        *([values] * (2 if whole else 1)),
        row_links,
        col_links,
        parent,
        *([after] if whole else []),
    )


def rows_kernel(own, other, own_links, other_links, out):
    window, width = out.shape[0], own.shape[1]
    for source, (values, links) in enumerate(((own, own_links), (other, other_links))):
        out[:, source * width:(source + 1) * width] = nn(
            one_hot(links[0], window), values[...]
        ).astype(bf16)


def spread_rows(own, other, row_links, window):
    return pl.pallas_call(
        rows_kernel,
        out_shape=jax.ShapeDtypeStruct((window, 2 * own.shape[1]), bf16),
        compiler_params=pltpu.CompilerParams(vmem_limit_bytes=VMEM_LIMIT),
        cost_estimate=pl.CostEstimate(
            flops=4 * window * own.size, bytes_accessed=12 * own.size, transcendentals=0
        ),
    )(own, other, *row_links)


def update_kernel(places, rows, own, other, own_links, other_links, total, *refs):
    out, cols = refs[-2:]
    window, width = cols.shape[0], own.shape[2]

    @pl.when(pl.program_id(1) == 0)
    def _():
        for source, (values, links) in enumerate(((own, own_links), (other, other_links))):
            cols[:, source * width:(source + 1) * width] = nn(
                one_hot(links[0, 0], window), values[0]
            ).astype(bf16)

    tile = out.shape[1]
    here = pl.ds(pl.multiple_of(pl.program_id(1) * tile, tile), tile)
    out[...] = total[...] - nt(rows[...], cols[here, :])


def update_windows(total, rows, own, other, places, col_links, after):
    window = total.shape[0]
    count, children, width = own.shape
    tile = largest_tile(window)
    block = pl.BlockSpec((1, children, width), lambda i, t, places: (i, 0, 0))
    link = pl.BlockSpec((1, 1, 1, children), lambda i, t, places: (places[i], 0, 0, 0))
    area = pl.BlockSpec(
        (window, tile), lambda i, t, places: (0, places[i] * (window // tile) + t)
    )
    return pl.pallas_call(
        update_kernel,
        out_shape=jax.ShapeDtypeStruct(total.shape, f32),
        grid_spec=pltpu.PrefetchScalarGridSpec(
            num_scalar_prefetch=1,
            grid=(count, window // tile),
            in_specs=[
                pl.BlockSpec((window, 2 * width), lambda i, t, places: (0, 0)),
                block,
                block,
                link,
                link,
                area,
            ]
            + [pl.BlockSpec(memory_space=pl.ANY)] * len(after),
            out_specs=area,
            scratch_shapes=[pltpu.VMEM((window, 2 * width), bf16)],
        ),
        input_output_aliases={6: 0},
        compiler_params=pltpu.CompilerParams(vmem_limit_bytes=VMEM_LIMIT),
        cost_estimate=pl.CostEstimate(
            flops=4 * count * window * width * (window + children),
            bytes_accessed=8 * count * window * window,
            transcendentals=0,
        ),
    )(places, rows, own, other, *col_links, total, *after)


def local(front_pivot, front_lower, front_rest, parent_front, relation):
    leaves, prows, pcols = (lax.axis_size(a) for a in ("leaf", "prow", "pcol"))
    position = lax.axis_index(ROWS)
    across = lax.axis_index("pcol")
    pivot_rows, lower_rows = front_pivot[0], front_lower[0]
    rest_rows, parent_rows = front_rest[0], parent_front[0]
    rows_here, pivot_order = pivot_rows.shape
    block_rows, child_order = rest_rows.shape
    window = parent_rows.shape[0]
    child_half = child_order // 2
    blocks = child_half // block_rows
    near = prows // 2
    leaf_index = lax.axis_index("leaf")
    side = leaf_index % 2
    partner = leaf_index + 1 - 2 * side

    def to_sibling(value):
        return lax.ppermute(value, "leaf", [(g, g ^ 1) for g in range(leaves)])

    def to_cols(value, apart, swap):
        pairs = [
            ((g * prows + r) * pcols + c, ((g ^ swap) * prows + r) * pcols + (c + apart) % pcols)
            for g in range(leaves)
            for r in range(prows)
            for c in range(pcols)
        ]
        return lax.ppermute(value, ("leaf",) + ROWS, pairs)

    def links_of(child):
        links = lax.dynamic_index_in_dim(relation, child, 0, keepdims=False)
        rows = lax.dynamic_slice_in_dim(links, position * block_rows, block_rows, 0)
        cols = lax.dynamic_slice_in_dim(links, side * child_half, child_half, 0)
        cols = cols.reshape(blocks, 1, 1, block_rows)
        first = side * blocks + jnp.arange(blocks, dtype=jnp.int32)
        return (
            (rows - position * window).reshape(1, 1, block_rows),
            cols - first.reshape(blocks, 1, 1, 1) * window,
        )

    own_row_links, own_col_links = links_of(leaf_index)
    other_row_links, other_col_links = links_of(partner)
    row_links = (own_row_links, other_row_links)
    col_links = (own_col_links, other_col_links)

    widths = panel_widths(pivot_order)
    starts = [sum(widths[:p]) for p in range(len(widths))]
    def along(value, step):
        return lax.ppermute(value, "prow", [(r, (r + step) % prows) for r in range(prows)])

    across_z = rows_here * pcols
    column_blocks = []
    spans = [(starts[0], starts[1]), (starts[1], starts[2]), (starts[2], pivot_order)]
    for n, (s, end) in enumerate(spans):
        mine = pivot_rows[:, s:end]
        if n == 0:
            mine = jnp.stack([mine] + [along(mine, step) for step in range(1, prows)])
        else:
            mine = lax.all_gather(mine, "prow", axis=0)[s // across_z:]
        column_blocks.append([mine] + [to_cols(mine, apart, 0) for apart in range(1, pcols)])

    def update(total, p, after):
        rounded, other, owns, others = panels[p]
        rows = spread_rows(rounded, other, row_links, window)
        for apart in range(pcols):
            places = jnp.arange(near, dtype=jnp.int32) * pcols + lax.rem(
                across - apart + pcols, pcols
            ).astype(jnp.int32)
            total = update_windows(
                total,
                rows,
                owns[apart],
                others[apart],
                places,
                col_links,
                () if apart else after,
            )
        return total

    own_block = (position - side * blocks).astype(jnp.int32)
    done, panels, lines = [], [], []
    place = jnp.stack([lax.axis_index("prow"), across, side]).astype(jnp.int32)

    def pass_on(p, side_now):
        rounded, other, line = lines[p]
        kept = lax.dynamic_slice_in_dim(line, side_now * near, near, 0)
        sent = lax.dynamic_slice_in_dim(line, (1 - side_now) * near, near, 0)
        owns = [to_cols(kept, apart, 0) if apart else kept for apart in range(pcols)]
        others = [to_cols(sent, apart, 1) for apart in range(pcols)]
        panels.append((rounded, other, owns, others))
        return (kept, sent), tuple(owns[1:] + others)

    parts = []
    for p, (s, w) in enumerate(zip(starts, widths)):
        n = min(p, len(spans) - 1)
        if p == 0:
            waits = (column_blocks[1][0],)
        elif p == 1:
            start_total, leaving = add_rest(
                parent_rows,
                rest_rows,
                jnp.stack([side.astype(jnp.int32), own_block]),
                own_row_links,
                own_col_links,
                done[0][0],
            )
            waits = (start_total, column_blocks[2][0])
        elif p == 2:
            total = add_rest(
                start_total,
                to_sibling(leaving),
                jnp.stack([jnp.zeros((), jnp.int32), own_block]),
                other_row_links,
                other_col_links,
                None,
            )
            waits = parts[0][1] + (total,)
        elif p == 3:
            total = update(total, 0, parts[1][0])
            waits = (total,)
        corner_at = (s // across_z - spans[n][0] // across_z, s - spans[n][0])
        pivot, lower, rounded, side_now = factor_panel(
            s, w, place, column_blocks[n], p == 0, corner_at, lower_rows, done, waits
        )
        done.append((pivot, lower))
        lines.append((rounded, to_sibling(rounded), lax.all_gather(rounded, "prow", axis=0)))
        if p:
            parts.append(pass_on(p - 1, side_now[0]))
    parts.append(pass_on(len(starts) - 1, side_now[0]))

    for p in range(1, len(starts)):
        total = update(total, p, parts[p][1] if p < len(starts) - 1 else ())

    factor_rows = jnp.concatenate(
        [
            lax.dynamic_slice_in_dim(
                jnp.concatenate([jnp.zeros((pivot_order - pivot.shape[0], w), f32), pivot], axis=0),
                position * rows_here,
                rows_here,
                0,
            )
            for s, w, (pivot, _) in zip(starts, widths, done)
        ],
        axis=1,
    )
    lower_out = jnp.concatenate([lower for _, lower in done], axis=1)
    return (factor_rows[None], lower_out[None], total[None])


def solution(mesh):
    whole = P("leaf", ROWS, None)
    return jax.shard_map(
        local,
        mesh=mesh,
        in_specs=(whole, whole, whole, whole, P()),
        out_specs=(whole, whole, whole),
        check_vma=False,
    )
```

```python
import math

import jax
import jax.numpy as jnp
from jax import lax
from jax.experimental import pallas as pl
from jax.experimental.pallas import tpu as pltpu
from jax.sharding import PartitionSpec as P

ROWS = ("prow", "pcol")
bf16 = jnp.bfloat16
f32 = jnp.float32
LANES = 128
SUBS = 8
GROUP = 32
TALL = 768
VMEM_LIMIT = 56 << 20


def panel_widths(order):
    narrow = order // 6
    return (narrow, 2 * narrow, 2 * narrow, narrow)


def split(x):
    top = x.astype(bf16)
    return top, (x - top.astype(f32)).astype(bf16)


def left_parts(x):
    top, low = split(x)
    return jnp.concatenate([top, top, low], axis=1)


def right_parts(x):
    top, low = split(x)
    return jnp.concatenate([top, low, top], axis=1)


def nt(a, b):
    return lax.dot_general(a, b, (((1,), (1,)), ((), ())), preferred_element_type=f32)


def nn(a, b):
    return jnp.dot(a, b, preferred_element_type=f32)


def spread_lane(x, lane):
    return jnp.broadcast_to(x[:, lane:lane + 1], (SUBS, LANES))


def spread_sub(x, sub):
    return jnp.broadcast_to(x[sub:sub + 1, :], (SUBS, LANES))


def factor_square(square):
    lane = lax.broadcasted_iota(jnp.int32, (SUBS, LANES), 1)
    sub = lax.broadcasted_iota(jnp.int32, (SUBS, LANES), 0)
    count = LANES // SUBS
    span = GROUP // SUBS
    state = [square[SUBS * r:SUBS * (r + 1), :] for r in range(count)]
    inverses = []
    for b in range(count):
        first = SUBS * b
        last = (b // span + 1) * span
        block = state[b]
        inside = (lane >= first) & (lane < first + SUBS)
        columns = [spread_lane(block, first + k) for k in range(SUBS)]
        d = [
            [spread_sub(columns[k], i) if k >= i else None for k in range(SUBS)]
            for i in range(SUBS)
        ]
        packed = jnp.where(inside, (lane - first == sub).astype(f32), block)
        rows = [spread_sub(packed, i) for i in range(SUBS)]
        follow = b + 1 < last
        if follow:
            ahead = state[b + 1]
            beside = [spread_lane(ahead, first + k) for k in range(SUBS)]
            ahead = jnp.where(inside, 0.0, ahead)
        scales, steps = [], []
        for i in range(SUBS):
            scale = lax.rsqrt(d[i][i])
            scales.append(scale)
            step = [d[i][k] * scale if k > i else None for k in range(SUBS)]
            steps.append(step)
            rows[i] = rows[i] * scale
            for k in range(i + 1, SUBS):
                for m in range(k, SUBS):
                    d[k][m] = d[k][m] - step[k] * step[m]
            for k in range(i + 1, SUBS):
                rows[k] = rows[k] - step[k] * rows[i]
            if follow:
                beside[i] = beside[i] * scale
                ahead = ahead - beside[i] * rows[i]
                for k in range(i + 1, SUBS):
                    beside[k] = beside[k] - step[k] * beside[i]
        whole = rows[0]
        for i in range(1, SUBS):
            whole = jnp.where(sub == i, rows[i], whole)
        inverses.append(whole)
        if follow:
            state[b + 1] = ahead
        if b + 2 < last:
            back = [None] * SUBS
            for i in reversed(range(SUBS)):
                total = rows[i]
                for k in range(i + 1, SUBS):
                    total = total - steps[i][k] * back[k]
                back[i] = total * scales[i]
            for r in range(b + 2, last):
                below = state[r]
                left = [spread_lane(below, first + k) for k in range(SUBS)]
                below = jnp.where(inside, 0.0, below)
                for k in range(SUBS):
                    below = below - left[k] * back[k]
                state[r] = below
        if b + 1 == last and last < count:
            start = GROUP * (b // span)
            solved = jnp.concatenate(
                [
                    jnp.where((lane >= SUBS * (g + 1)) & (lane < SUBS * last), 0.0, inverses[g])
                    for g in range(b + 1 - span, b + 1)
                ],
                axis=0,
            )
            after = jnp.concatenate(state[last:], axis=0)
            own = slice(start, start + GROUP)
            left = nt(left_parts(after[:, own]), right_parts(solved[:, own]))
            top, low = split(solved)
            change = nn(left_parts(left), jnp.concatenate([top, low, top], axis=0))
            for r in range(last, count):
                at = SUBS * (r - last)
                done = (lane >= start) & (lane < start + GROUP)
                state[r] = jnp.where(done, 0.0, state[r]) - change[at:at + SUBS, :]
    return jnp.concatenate(
        [jnp.where(lane < SUBS * (b + 1), inverses[b], 0.0) for b in range(count)], axis=0
    )


def largest_tile(rows):
    return next(t for t in (256, 128, 64, 32, 16, 8) if rows % t == 0)


def tall_tile(rows):
    return next(rows // n for n in range(1, rows) if rows % n == 0 and rows // n <= TALL)


def panel_kernel(first, base, bases, pcols, turned, corner_at, *refs):
    refs = list(refs)
    place, shares, refs = refs[0], refs[1:1 + pcols], refs[1 + pcols:]
    before = len(bases)
    earlier = [(refs[2 * q], refs[2 * q + 1]) for q in range(before)]
    refs = refs[2 * before:]
    waits = len(refs) - 5 - before
    lower_in = refs[0]
    pivot, lower, rounded, side, tops = refs[waits:waits + 5]
    crowns = refs[waits + 5:]
    side[0] = place[2]
    width = pivot.shape[1]
    count = width // LANES
    skip = first - base
    bottom = skip + width
    for q in range(before):
        for t in range(count):
            at = first - bases[q] + t * LANES
            crowns[q][t * LANES:(t + 1) * LANES, :] = right_parts(
                earlier[q][0][at:at + LANES, :]
            )
    low, left = corner_at
    prows, share_rows = shares[0].shape[:2]
    for apart in range(pcols):
        source = lax.rem(place[1] - apart + pcols, pcols)
        for r in range(prows - low):
            line = lax.rem(place[0] - r + prows, prows) if turned else r
            at = pl.multiple_of((line * pcols + source) * share_rows, 8)
            pivot[pl.ds(at, share_rows), :] = shares[apart][low + r, :, left:left + width]
    pltpu.sync_copy(lower_in.at[:, first:first + width], lower)

    def subtract(target, pasts, offsets):
        tile = tall_tile(target.shape[0])

        @pl.loop(0, target.shape[0] // tile)
        def _(t):
            at = pl.multiple_of(t * tile, tile)
            values = target[pl.ds(at, tile), :]
            for q in range(before):
                past = pasts[q][pl.ds(pl.multiple_of(offsets[q] + at, 8), tile), :]
                values = values - nt(left_parts(past), crowns[q][...])
            target[pl.ds(at, tile), :] = values

    if before:
        subtract(pivot, [past for past, _ in earlier], [base - b for b in bases])
        subtract(lower, [past for _, past in earlier], [0] * before)
    if skip:
        pivot[0:skip, :] = jnp.zeros((skip, width), f32)

    row = lax.broadcasted_iota(jnp.int32, (width, LANES), 0)
    lane = lax.broadcasted_iota(jnp.int32, (width, LANES), 1)

    @pl.loop(0, count)
    def _(k):
        here = pl.ds(pl.multiple_of(k * LANES, LANES), LANES)
        corner = pl.ds(pl.multiple_of(skip + k * LANES, LANES), LANES)
        solver = right_parts(factor_square(pivot[corner, here]))
        solved = nt(left_parts(pivot[skip:bottom, here]), solver)
        solved = jnp.where(row - k * LANES >= lane, solved, 0.0)
        pivot[skip:bottom, here] = solved
        solved = jnp.where(row >= (k + 1) * LANES, solved, 0.0)
        tops[...] = right_parts(solved)
        if count > 1:
            pivot[skip:bottom, LANES:] -= nt(left_parts(solved), tops[LANES:, :])

        def run(ref, start, rows):
            tile = tall_tile(rows)

            @pl.loop(0, rows // tile)
            def _(t):
                band = pl.ds(pl.multiple_of(start + t * tile, 8), tile)
                solved = nt(left_parts(ref[band, here]), solver)
                ref[band, here] = solved
                if count > 1:
                    ref[band, LANES:] -= nt(left_parts(solved), tops[LANES:, :])

        if pivot.shape[0] > bottom:
            run(pivot, bottom, pivot.shape[0] - bottom)
        run(lower, 0, lower.shape[0])

    tile = largest_tile(lower.shape[0])

    @pl.loop(0, lower.shape[0] // tile)
    def _(t):
        here = pl.ds(pl.multiple_of(t * tile, tile), tile)
        rounded[here, :] = lower[here, :].astype(bf16)


def factor_panel(first, width, place, shares, turned, corner_at, lower, earlier, after):
    prows, share_rows, _ = shares[0].shape
    rows = len(shares) * (prows - corner_at[0]) * share_rows
    order = lower.shape[1]
    base = order - rows
    flat = [past for pair in earlier for past in pair]
    in_vmem = pl.BlockSpec(memory_space=pltpu.VMEM)
    anywhere = pl.BlockSpec(memory_space=pl.ANY)
    bases = [order - past.shape[0] for past, _ in earlier]
    return pl.pallas_call(
        lambda *refs: panel_kernel(first, base, bases, len(shares), turned, corner_at, *refs),
        out_shape=(
            jax.ShapeDtypeStruct((rows, width), f32),
            jax.ShapeDtypeStruct((lower.shape[0], width), f32),
            jax.ShapeDtypeStruct((lower.shape[0], width), bf16),
            jax.ShapeDtypeStruct((1,), jnp.int32),
        ),
        in_specs=[pl.BlockSpec(memory_space=pltpu.SMEM)]
        + [in_vmem] * (len(shares) + len(flat))
        + [anywhere] * (1 + len(after)),
        out_specs=[in_vmem] * 3 + [pl.BlockSpec(memory_space=pltpu.SMEM)],
        scratch_shapes=[pltpu.VMEM((width, 3 * LANES), bf16)]
        + [pltpu.VMEM((width, 3 * past.shape[1]), bf16) for past, _ in earlier],
        compiler_params=pltpu.CompilerParams(vmem_limit_bytes=VMEM_LIMIT),
        cost_estimate=pl.CostEstimate(
            flops=width * 50000000,
            bytes_accessed=10 * width * (rows + lower.shape[0]),
            transcendentals=0,
        ),
    )(place, *shares, *flat, lower, *after)


def one_hot(links, window):
    places = lax.broadcasted_iota(jnp.int32, (window, links.shape[1]), 0)
    return (places == links).astype(bf16)


def rest_kernel(whole, half, values, *refs):
    out, table, placed = refs[-3:]
    if whole:
        out, leaving = refs[-4:-2]
        leaving[...] = refs[0][...]
        refs = refs[1:]
    row_links, col_links, parent = refs[:3]
    window = out.shape[0]
    rows = values.shape[0]

    @pl.when(pl.program_id(0) == 0)
    def _():
        spread = one_hot(row_links[0], window)
        table[:, :rows] = spread
        table[:, rows:] = spread

    tile = largest_tile(out.shape[1])
    count = col_links.shape[0]
    step = pl.program_id(0)
    mine = (half[1] >= step * count) & (half[1] < (step + 1) * count)

    def spread_of(part, at, depth):
        for i in range(count):
            spread = one_hot(col_links[i, 0], window)
            block, area = slice(i * rows, (i + 1) * rows), slice(i * window, (i + 1) * window)
            placed[at:at + rows, area] = nt(part[:, block], spread).astype(bf16)
        if depth:

            @pl.loop(0, out.shape[1] // tile)
            def _(t):
                here = pl.ds(pl.multiple_of(t * tile, tile), tile)
                out[:, here] = parent[:, here] + nn(table[:, :depth], placed[:depth, here])

    @pl.when(mine)
    def _():
        top, low = split(values[...])
        spread_of(top, 0, 0)
        spread_of(low, rows, 2 * rows)

    @pl.when(jnp.logical_not(mine))
    def _():
        spread_of(values[...].astype(bf16), 0, rows)


def add_rest(parent, values, half, row_links, col_links, after, whole):
    window = parent.shape[0]
    rows = values.shape[0]
    group = LANES // math.gcd(LANES, rows)
    steps = parent.shape[1] // window // group
    area = pl.BlockSpec((window, group * window), lambda w, half: (0, w))
    block = (rows, group * rows)
    total = jax.ShapeDtypeStruct(parent.shape, f32)
    crossing = [pl.BlockSpec(block, lambda w, half: (0, (1 - half[0]) * steps + w))]
    leaving = pl.BlockSpec(block, lambda w, half: (0, w))
    return pl.pallas_call(
        lambda *refs: rest_kernel(whole, *refs),
        out_shape=(total, jax.ShapeDtypeStruct((rows, values.shape[1] // 2), f32)) if whole else total,
        grid_spec=pltpu.PrefetchScalarGridSpec(
            num_scalar_prefetch=1,
            grid=(steps,),
            in_specs=[pl.BlockSpec(block, lambda w, half: (0, half[0] * steps + w))]
            + (crossing if whole else [])
            + [
                pl.BlockSpec((1, 1, rows), lambda w, half: (0, 0, 0)),
                pl.BlockSpec((group, 1, 1, rows), lambda w, half: (w, 0, 0, 0)),
                area,
            ]
            + [pl.BlockSpec(memory_space=pl.ANY)] * len(after),
            out_specs=(area, leaving) if whole else area,
            scratch_shapes=[
                pltpu.VMEM((window, 2 * rows), bf16),
                pltpu.VMEM((2 * rows, group * window), bf16),
            ],
        ),
        input_output_aliases={} if whole else {4: 0},
        compiler_params=pltpu.CompilerParams(vmem_limit_bytes=VMEM_LIMIT),
        cost_estimate=pl.CostEstimate(
            flops=4 * rows * parent.size + 4 * rows * rows * parent.shape[1],
            bytes_accessed=8 * parent.size + 4 * rows * rows * steps * group,
            transcendentals=0,
        ),
    )(
        half,
        *([values] * (2 if whole else 1)),
        row_links,
        col_links,
        parent,
        *after,
    )


def rows_kernel(own, other, own_links, other_links, out):
    window, width = out.shape[0], own.shape[1]
    for source, (values, links) in enumerate(((own, own_links), (other, other_links))):
        out[:, source * width:(source + 1) * width] = nn(
            one_hot(links[0], window), values[...]
        ).astype(bf16)


def spread_rows(own, other, row_links, window):
    return pl.pallas_call(
        rows_kernel,
        out_shape=jax.ShapeDtypeStruct((window, 2 * own.shape[1]), bf16),
        compiler_params=pltpu.CompilerParams(vmem_limit_bytes=VMEM_LIMIT),
        cost_estimate=pl.CostEstimate(
            flops=4 * window * own.size, bytes_accessed=12 * own.size, transcendentals=0
        ),
    )(own, other, *row_links)


def update_kernel(places, rows, own, other, own_links, other_links, total, *refs):
    out, cols = refs[-2:]
    window, width = cols.shape[0], own.shape[2]

    @pl.when(pl.program_id(1) == 0)
    def _():
        for source, (values, links) in enumerate(((own, own_links), (other, other_links))):
            cols[:, source * width:(source + 1) * width] = nn(
                one_hot(links[0, 0], window), values[0]
            ).astype(bf16)

    tile = out.shape[1]
    here = pl.ds(pl.multiple_of(pl.program_id(1) * tile, tile), tile)
    out[...] = total[...] - nt(rows[...], cols[here, :])


def update_windows(total, rows, own, other, places, col_links, after):
    window = total.shape[0]
    count, children, width = own.shape
    tile = largest_tile(window)
    block = pl.BlockSpec((1, children, width), lambda i, t, places: (i, 0, 0))
    link = pl.BlockSpec((1, 1, 1, children), lambda i, t, places: (places[i], 0, 0, 0))
    area = pl.BlockSpec(
        (window, tile), lambda i, t, places: (0, places[i] * (window // tile) + t)
    )
    return pl.pallas_call(
        update_kernel,
        out_shape=jax.ShapeDtypeStruct(total.shape, f32),
        grid_spec=pltpu.PrefetchScalarGridSpec(
            num_scalar_prefetch=1,
            grid=(count, window // tile),
            in_specs=[
                pl.BlockSpec((window, 2 * width), lambda i, t, places: (0, 0)),
                block,
                block,
                link,
                link,
                area,
            ]
            + [pl.BlockSpec(memory_space=pl.ANY)] * len(after),
            out_specs=area,
            scratch_shapes=[pltpu.VMEM((window, 2 * width), bf16)],
        ),
        input_output_aliases={6: 0},
        compiler_params=pltpu.CompilerParams(vmem_limit_bytes=VMEM_LIMIT),
        cost_estimate=pl.CostEstimate(
            flops=4 * count * window * width * (window + children),
            bytes_accessed=8 * count * window * window,
            transcendentals=0,
        ),
    )(places, rows, own, other, *col_links, total, *after)


def local(front_pivot, front_lower, front_rest, parent_front, relation):
    leaves, prows, pcols = (lax.axis_size(a) for a in ("leaf", "prow", "pcol"))
    position = lax.axis_index(ROWS)
    across = lax.axis_index("pcol")
    pivot_rows, lower_rows = front_pivot[0], front_lower[0]
    rest_rows, parent_rows = front_rest[0], parent_front[0]
    rows_here, pivot_order = pivot_rows.shape
    block_rows, child_order = rest_rows.shape
    window = parent_rows.shape[0]
    child_half = child_order // 2
    blocks = child_half // block_rows
    near = prows // 2
    leaf_index = lax.axis_index("leaf")
    side = leaf_index % 2
    partner = leaf_index + 1 - 2 * side

    def to_sibling(value):
        return lax.ppermute(value, "leaf", [(g, g ^ 1) for g in range(leaves)])

    def to_cols(value, apart, swap):
        pairs = [
            ((g * prows + r) * pcols + c, ((g ^ swap) * prows + r) * pcols + (c + apart) % pcols)
            for g in range(leaves)
            for r in range(prows)
            for c in range(pcols)
        ]
        return lax.ppermute(value, ("leaf",) + ROWS, pairs)

    def links_of(child):
        links = lax.dynamic_index_in_dim(relation, child, 0, keepdims=False)
        rows = lax.dynamic_slice_in_dim(links, position * block_rows, block_rows, 0)
        cols = lax.dynamic_slice_in_dim(links, side * child_half, child_half, 0)
        cols = cols.reshape(blocks, 1, 1, block_rows)
        first = side * blocks + jnp.arange(blocks, dtype=jnp.int32)
        return (
            (rows - position * window).reshape(1, 1, block_rows),
            cols - first.reshape(blocks, 1, 1, 1) * window,
        )

    own_row_links, own_col_links = links_of(leaf_index)
    other_row_links, other_col_links = links_of(partner)
    row_links = (own_row_links, other_row_links)
    col_links = (own_col_links, other_col_links)

    widths = panel_widths(pivot_order)
    starts = [sum(widths[:p]) for p in range(len(widths))]
    def along(value, step):
        return lax.ppermute(value, "prow", [(r, (r + step) % prows) for r in range(prows)])

    across_z = rows_here * pcols
    column_blocks = []
    spans = [(starts[0], starts[1]), (starts[1], starts[2]), (starts[2], pivot_order)]
    for n, (s, end) in enumerate(spans):
        mine = pivot_rows[:, s:end]
        if n == 0:
            mine = jnp.stack([mine] + [along(mine, step) for step in range(1, prows)])
        else:
            mine = lax.all_gather(mine, "prow", axis=0)[s // across_z:]
        column_blocks.append([mine] + [to_cols(mine, apart, 0) for apart in range(1, pcols)])

    def update(total, p, before_first, before_last):
        rounded, other, owns, others = panels[p]
        rows = spread_rows(rounded, other, row_links, window)
        for apart in range(pcols):
            places = jnp.arange(near, dtype=jnp.int32) * pcols + lax.rem(
                across - apart + pcols, pcols
            ).astype(jnp.int32)
            total = update_windows(
                total,
                rows,
                owns[apart],
                others[apart],
                places,
                col_links,
                before_last if apart == pcols - 1 else () if apart else before_first,
            )
        return total

    own_block = (position - side * blocks).astype(jnp.int32)
    done, panels, lines = [], [], []
    place = jnp.stack([lax.axis_index("prow"), across, side]).astype(jnp.int32)

    def pass_on(p, side_now):
        rounded, other, line = lines[p]
        kept = lax.dynamic_slice_in_dim(line, side_now * near, near, 0)
        sent = lax.dynamic_slice_in_dim(line, (1 - side_now) * near, near, 0)
        owns = [to_cols(kept, apart, 0) if apart else kept for apart in range(pcols)]
        others = [to_cols(sent, apart, 1) for apart in range(pcols)]
        panels.append((rounded, other, owns, others))
        return (kept, sent), tuple(owns[1:] + others)

    parts = []
    for p, (s, w) in enumerate(zip(starts, widths)):
        n = min(p, len(spans) - 1)
        if p == 0:
            start_total, leaving = add_rest(
                parent_rows,
                rest_rows,
                jnp.stack([side.astype(jnp.int32), own_block]),
                own_row_links,
                own_col_links,
                (column_blocks[0][-1], column_blocks[1][0]),
                True,
            )
            waits = (start_total, column_blocks[2][0])
        elif p == 2:
            waits = parts[0][1]
        elif p == 3:
            total = add_rest(
                start_total,
                to_sibling(leaving),
                jnp.stack([jnp.zeros((), jnp.int32), own_block]),
                other_row_links,
                other_col_links,
                (),
                False,
            )
            total = update(total, 0, parts[1][0], ())
            waits = (total,)
        corner_at = (s // across_z - spans[n][0] // across_z, s - spans[n][0])
        pivot, lower, rounded, side_now = factor_panel(
            s, w, place, column_blocks[n], p == 0, corner_at, lower_rows, done, waits
        )
        done.append((pivot, lower))
        lines.append((rounded, to_sibling(rounded), lax.all_gather(rounded, "prow", axis=0)))
        if p:
            parts.append(pass_on(p - 1, side_now[0]))
    parts.append(pass_on(len(starts) - 1, side_now[0]))

    for p in range(1, len(starts)):
        total = update(total, p, parts[p][1] if p == 1 else (), ())

    factor_rows = jnp.concatenate(
        [
            lax.dynamic_slice_in_dim(
                jnp.concatenate([jnp.zeros((pivot_order - pivot.shape[0], w), f32), pivot], axis=0),
                position * rows_here,
                rows_here,
                0,
            )
            for s, w, (pivot, _) in zip(starts, widths, done)
        ],
        axis=1,
    )
    lower_out = jnp.concatenate([lower for _, lower in done], axis=1)
    return (factor_rows[None], lower_out[None], total[None])


def solution(mesh):
    whole = P("leaf", ROWS, None)
    return jax.shard_map(
        local,
        mesh=mesh,
        in_specs=(whole, whole, whole, whole, P()),
        out_specs=(whole, whole, whole),
        check_vma=False,
    )
```

```python
import math

import jax
import jax.numpy as jnp
from jax import lax
from jax.experimental import pallas as pl
from jax.experimental.pallas import tpu as pltpu
from jax.sharding import PartitionSpec as P

ROWS = ("prow", "pcol")
bf16 = jnp.bfloat16
f32 = jnp.float32
LANES = 128
SUBS = 8
GROUP = 32
TALL = 768
VMEM_LIMIT = 56 << 20


def panel_widths(order):
    narrow = order // 6
    return (narrow, 2 * narrow, 2 * narrow, narrow)


def split(x):
    top = x.astype(bf16)
    return top, (x - top.astype(f32)).astype(bf16)


def left_parts(x):
    top, low = split(x)
    return jnp.concatenate([top, top, low], axis=1)


def right_parts(x):
    top, low = split(x)
    return jnp.concatenate([top, low, top], axis=1)


def nt(a, b):
    return lax.dot_general(a, b, (((1,), (1,)), ((), ())), preferred_element_type=f32)


def nn(a, b):
    return jnp.dot(a, b, preferred_element_type=f32)


def spread_lane(x, lane):
    return jnp.broadcast_to(x[:, lane:lane + 1], (SUBS, LANES))


def spread_sub(x, sub):
    return jnp.broadcast_to(x[sub:sub + 1, :], (SUBS, LANES))


def factor_square(square):
    lane = lax.broadcasted_iota(jnp.int32, (SUBS, LANES), 1)
    sub = lax.broadcasted_iota(jnp.int32, (SUBS, LANES), 0)
    count = LANES // SUBS
    span = GROUP // SUBS
    state = [square[SUBS * r:SUBS * (r + 1), :] for r in range(count)]
    inverses = []
    for b in range(count):
        first = SUBS * b
        last = (b // span + 1) * span
        block = state[b]
        inside = (lane >= first) & (lane < first + SUBS)
        columns = [spread_lane(block, first + k) for k in range(SUBS)]
        d = [
            [spread_sub(columns[k], i) if k >= i else None for k in range(SUBS)]
            for i in range(SUBS)
        ]
        packed = jnp.where(inside, (lane - first == sub).astype(f32), block)
        rows = [spread_sub(packed, i) for i in range(SUBS)]
        follow = b + 1 < last
        if follow:
            ahead = state[b + 1]
            beside = [spread_lane(ahead, first + k) for k in range(SUBS)]
            ahead = jnp.where(inside, 0.0, ahead)
        scales, steps = [], []
        for i in range(SUBS):
            scale = lax.rsqrt(d[i][i])
            scales.append(scale)
            step = [d[i][k] * scale if k > i else None for k in range(SUBS)]
            steps.append(step)
            rows[i] = rows[i] * scale
            for k in range(i + 1, SUBS):
                for m in range(k, SUBS):
                    d[k][m] = d[k][m] - step[k] * step[m]
            for k in range(i + 1, SUBS):
                rows[k] = rows[k] - step[k] * rows[i]
            if follow:
                beside[i] = beside[i] * scale
                ahead = ahead - beside[i] * rows[i]
                for k in range(i + 1, SUBS):
                    beside[k] = beside[k] - step[k] * beside[i]
        whole = rows[0]
        for i in range(1, SUBS):
            whole = jnp.where(sub == i, rows[i], whole)
        inverses.append(whole)
        if follow:
            state[b + 1] = ahead
        if b + 2 < last:
            back = [None] * SUBS
            for i in reversed(range(SUBS)):
                total = rows[i]
                for k in range(i + 1, SUBS):
                    total = total - steps[i][k] * back[k]
                back[i] = total * scales[i]
            for r in range(b + 2, last):
                below = state[r]
                left = [spread_lane(below, first + k) for k in range(SUBS)]
                below = jnp.where(inside, 0.0, below)
                for k in range(SUBS):
                    below = below - left[k] * back[k]
                state[r] = below
        if b + 1 == last and last < count:
            start = GROUP * (b // span)
            solved = jnp.concatenate(
                [
                    jnp.where((lane >= SUBS * (g + 1)) & (lane < SUBS * last), 0.0, inverses[g])
                    for g in range(b + 1 - span, b + 1)
                ],
                axis=0,
            )
            after = jnp.concatenate(state[last:], axis=0)
            own = slice(start, start + GROUP)
            left = nt(left_parts(after[:, own]), right_parts(solved[:, own]))
            top, low = split(solved)
            change = nn(left_parts(left), jnp.concatenate([top, low, top], axis=0))
            for r in range(last, count):
                at = SUBS * (r - last)
                done = (lane >= start) & (lane < start + GROUP)
                state[r] = jnp.where(done, 0.0, state[r]) - change[at:at + SUBS, :]
    return jnp.concatenate(
        [jnp.where(lane < SUBS * (b + 1), inverses[b], 0.0) for b in range(count)], axis=0
    )


def largest_tile(rows):
    return next(t for t in (256, 128, 64, 32, 16, 8) if rows % t == 0)


def tall_tile(rows):
    return next(rows // n for n in range(1, rows) if rows % n == 0 and rows // n <= TALL)


def panel_kernel(first, base, bases, pcols, turned, corner_at, *refs):
    refs = list(refs)
    place, shares, refs = refs[0], refs[1:1 + pcols], refs[1 + pcols:]
    before = len(bases)
    earlier = [(refs[2 * q], refs[2 * q + 1]) for q in range(before)]
    refs = refs[2 * before:]
    waits = len(refs) - 5 - before
    lower_in = refs[0]
    pivot, lower, rounded, side, tops = refs[waits:waits + 5]
    crowns = refs[waits + 5:]
    side[0] = place[2]
    width = pivot.shape[1]
    count = width // LANES
    skip = first - base
    bottom = skip + width
    for q in range(before):
        for t in range(count):
            at = first - bases[q] + t * LANES
            crowns[q][t * LANES:(t + 1) * LANES, :] = right_parts(
                earlier[q][0][at:at + LANES, :]
            )
    low, left = corner_at
    prows, share_rows = shares[0].shape[:2]
    for apart in range(pcols):
        source = lax.rem(place[1] - apart + pcols, pcols)
        for r in range(prows - low):
            line = lax.rem(place[0] - r + prows, prows) if turned else r
            at = pl.multiple_of((line * pcols + source) * share_rows, 8)
            pivot[pl.ds(at, share_rows), :] = shares[apart][low + r, :, left:left + width]
    pltpu.sync_copy(lower_in.at[:, first:first + width], lower)

    def subtract(target, pasts, offsets):
        tile = tall_tile(target.shape[0])

        @pl.loop(0, target.shape[0] // tile)
        def _(t):
            at = pl.multiple_of(t * tile, tile)
            values = target[pl.ds(at, tile), :]
            for q in range(before):
                past = pasts[q][pl.ds(pl.multiple_of(offsets[q] + at, 8), tile), :]
                values = values - nt(left_parts(past), crowns[q][...])
            target[pl.ds(at, tile), :] = values

    if before:
        subtract(pivot, [past for past, _ in earlier], [base - b for b in bases])
        subtract(lower, [past for _, past in earlier], [0] * before)
    if skip:
        pivot[0:skip, :] = jnp.zeros((skip, width), f32)

    row = lax.broadcasted_iota(jnp.int32, (width, LANES), 0)
    lane = lax.broadcasted_iota(jnp.int32, (width, LANES), 1)

    @pl.loop(0, count)
    def _(k):
        here = pl.ds(pl.multiple_of(k * LANES, LANES), LANES)
        corner = pl.ds(pl.multiple_of(skip + k * LANES, LANES), LANES)
        solver = right_parts(factor_square(pivot[corner, here]))
        solved = nt(left_parts(pivot[skip:bottom, here]), solver)
        solved = jnp.where(row - k * LANES >= lane, solved, 0.0)
        pivot[skip:bottom, here] = solved
        solved = jnp.where(row >= (k + 1) * LANES, solved, 0.0)
        tops[...] = right_parts(solved)
        if count > 1:
            pivot[skip:bottom, LANES:] -= nt(left_parts(solved), tops[LANES:, :])

        def run(ref, start, rows):
            tile = tall_tile(rows)

            @pl.loop(0, rows // tile)
            def _(t):
                band = pl.ds(pl.multiple_of(start + t * tile, 8), tile)
                solved = nt(left_parts(ref[band, here]), solver)
                ref[band, here] = solved
                if count > 1:
                    ref[band, LANES:] -= nt(left_parts(solved), tops[LANES:, :])

        if pivot.shape[0] > bottom:
            run(pivot, bottom, pivot.shape[0] - bottom)
        run(lower, 0, lower.shape[0])

    tile = largest_tile(lower.shape[0])

    @pl.loop(0, lower.shape[0] // tile)
    def _(t):
        here = pl.ds(pl.multiple_of(t * tile, tile), tile)
        rounded[here, :] = lower[here, :].astype(bf16)


def factor_panel(first, width, place, shares, turned, corner_at, lower, earlier, after):
    prows, share_rows, _ = shares[0].shape
    rows = len(shares) * (prows - corner_at[0]) * share_rows
    order = lower.shape[1]
    base = order - rows
    flat = [past for pair in earlier for past in pair]
    in_vmem = pl.BlockSpec(memory_space=pltpu.VMEM)
    anywhere = pl.BlockSpec(memory_space=pl.ANY)
    bases = [order - past.shape[0] for past, _ in earlier]
    return pl.pallas_call(
        lambda *refs: panel_kernel(first, base, bases, len(shares), turned, corner_at, *refs),
        out_shape=(
            jax.ShapeDtypeStruct((rows, width), f32),
            jax.ShapeDtypeStruct((lower.shape[0], width), f32),
            jax.ShapeDtypeStruct((lower.shape[0], width), bf16),
            jax.ShapeDtypeStruct((1,), jnp.int32),
        ),
        in_specs=[pl.BlockSpec(memory_space=pltpu.SMEM)]
        + [in_vmem] * (len(shares) + len(flat))
        + [anywhere] * (1 + len(after)),
        out_specs=[in_vmem] * 3 + [pl.BlockSpec(memory_space=pltpu.SMEM)],
        scratch_shapes=[pltpu.VMEM((width, 3 * LANES), bf16)]
        + [pltpu.VMEM((width, 3 * past.shape[1]), bf16) for past, _ in earlier],
        compiler_params=pltpu.CompilerParams(vmem_limit_bytes=VMEM_LIMIT),
        cost_estimate=pl.CostEstimate(
            flops=width * 50000000,
            bytes_accessed=10 * width * (rows + lower.shape[0]),
            transcendentals=0,
        ),
    )(place, *shares, *flat, lower, *after)


def one_hot(links, window):
    places = lax.broadcasted_iota(jnp.int32, (window, links.shape[1]), 0)
    return (places == links).astype(bf16)


def rest_kernel(whole, half, values, *refs):
    out, table, placed = refs[-3:]
    if whole:
        out, leaving = refs[-4:-2]
        leaving[...] = refs[0][...]
        refs = refs[1:]
    row_links, col_links, parent = refs[:3]
    window = out.shape[0]
    rows = values.shape[0]

    @pl.when(pl.program_id(0) == 0)
    def _():
        spread = one_hot(row_links[0], window)
        table[:, :rows] = spread
        table[:, rows:] = spread

    tile = largest_tile(out.shape[1])
    count = col_links.shape[0]
    step = pl.program_id(0)
    mine = (half[1] >= step * count) & (half[1] < (step + 1) * count)

    def spread_of(part, at, depth):
        for i in range(count):
            spread = one_hot(col_links[i, 0], window)
            block, area = slice(i * rows, (i + 1) * rows), slice(i * window, (i + 1) * window)
            placed[at:at + rows, area] = nt(part[:, block], spread).astype(bf16)
        if depth:

            @pl.loop(0, out.shape[1] // tile)
            def _(t):
                here = pl.ds(pl.multiple_of(t * tile, tile), tile)
                out[:, here] = parent[:, here] + nn(table[:, :depth], placed[:depth, here])

    @pl.when(mine)
    def _():
        top, low = split(values[...])
        spread_of(top, 0, 0)
        spread_of(low, rows, 2 * rows)

    @pl.when(jnp.logical_not(mine))
    def _():
        spread_of(values[...].astype(bf16), 0, rows)


def add_rest(parent, values, half, row_links, col_links, after, whole):
    window = parent.shape[0]
    rows = values.shape[0]
    group = LANES // math.gcd(LANES, rows)
    steps = parent.shape[1] // window // group
    area = pl.BlockSpec((window, group * window), lambda w, half: (0, w))
    block = (rows, group * rows)
    total = jax.ShapeDtypeStruct(parent.shape, f32)
    crossing = [pl.BlockSpec(block, lambda w, half: (0, (1 - half[0]) * steps + w))]
    leaving = pl.BlockSpec(block, lambda w, half: (0, w))
    return pl.pallas_call(
        lambda *refs: rest_kernel(whole, *refs),
        out_shape=(total, jax.ShapeDtypeStruct((rows, values.shape[1] // 2), f32)) if whole else total,
        grid_spec=pltpu.PrefetchScalarGridSpec(
            num_scalar_prefetch=1,
            grid=(steps,),
            in_specs=[pl.BlockSpec(block, lambda w, half: (0, half[0] * steps + w))]
            + (crossing if whole else [])
            + [
                pl.BlockSpec((1, 1, rows), lambda w, half: (0, 0, 0)),
                pl.BlockSpec((group, 1, 1, rows), lambda w, half: (w, 0, 0, 0)),
                area,
            ]
            + [pl.BlockSpec(memory_space=pl.ANY)] * len(after),
            out_specs=(area, leaving) if whole else area,
            scratch_shapes=[
                pltpu.VMEM((window, 2 * rows), bf16),
                pltpu.VMEM((2 * rows, group * window), bf16),
            ],
        ),
        input_output_aliases={} if whole else {4: 0},
        compiler_params=pltpu.CompilerParams(vmem_limit_bytes=VMEM_LIMIT),
        cost_estimate=pl.CostEstimate(
            flops=4 * rows * parent.size + 4 * rows * rows * parent.shape[1],
            bytes_accessed=8 * parent.size + 4 * rows * rows * steps * group,
            transcendentals=0,
        ),
    )(
        half,
        *([values] * (2 if whole else 1)),
        row_links,
        col_links,
        parent,
        *after,
    )


def rows_kernel(own, other, own_links, other_links, out):
    window, width = out.shape[0], own.shape[1]
    for source, (values, links) in enumerate(((own, own_links), (other, other_links))):
        out[:, source * width:(source + 1) * width] = nn(
            one_hot(links[0], window), values[...]
        ).astype(bf16)


def spread_rows(own, other, row_links, window):
    return pl.pallas_call(
        rows_kernel,
        out_shape=jax.ShapeDtypeStruct((window, 2 * own.shape[1]), bf16),
        compiler_params=pltpu.CompilerParams(vmem_limit_bytes=VMEM_LIMIT),
        cost_estimate=pl.CostEstimate(
            flops=4 * window * own.size, bytes_accessed=12 * own.size, transcendentals=0
        ),
    )(own, other, *row_links)


def update_kernel(places, rows, own, other, own_links, other_links, total, *refs):
    out, cols = refs[-2:]
    window, width = cols.shape[0], own.shape[2]

    @pl.when(pl.program_id(1) == 0)
    def _():
        for source, (values, links) in enumerate(((own, own_links), (other, other_links))):
            cols[:, source * width:(source + 1) * width] = nn(
                one_hot(links[0, 0], window), values[0]
            ).astype(bf16)

    tile = out.shape[1]
    here = pl.ds(pl.multiple_of(pl.program_id(1) * tile, tile), tile)
    out[...] = total[...] - nt(rows[...], cols[here, :])


def update_windows(total, rows, own, other, places, col_links, after):
    window = total.shape[0]
    count, children, width = own.shape
    tile = largest_tile(window)
    block = pl.BlockSpec((1, children, width), lambda i, t, places: (i, 0, 0))
    link = pl.BlockSpec((1, 1, 1, children), lambda i, t, places: (places[i], 0, 0, 0))
    area = pl.BlockSpec(
        (window, tile), lambda i, t, places: (0, places[i] * (window // tile) + t)
    )
    return pl.pallas_call(
        update_kernel,
        out_shape=jax.ShapeDtypeStruct(total.shape, f32),
        grid_spec=pltpu.PrefetchScalarGridSpec(
            num_scalar_prefetch=1,
            grid=(count, window // tile),
            in_specs=[
                pl.BlockSpec((window, 2 * width), lambda i, t, places: (0, 0)),
                block,
                block,
                link,
                link,
                area,
            ]
            + [pl.BlockSpec(memory_space=pl.ANY)] * len(after),
            out_specs=area,
            scratch_shapes=[pltpu.VMEM((window, 2 * width), bf16)],
        ),
        input_output_aliases={6: 0},
        compiler_params=pltpu.CompilerParams(vmem_limit_bytes=VMEM_LIMIT),
        cost_estimate=pl.CostEstimate(
            flops=4 * count * window * width * (window + children),
            bytes_accessed=8 * count * window * window,
            transcendentals=0,
        ),
    )(places, rows, own, other, *col_links, total, *after)


def local(front_pivot, front_lower, front_rest, parent_front, relation):
    leaves, prows, pcols = (lax.axis_size(a) for a in ("leaf", "prow", "pcol"))
    position = lax.axis_index(ROWS)
    across = lax.axis_index("pcol")
    pivot_rows, lower_rows = front_pivot[0], front_lower[0]
    rest_rows, parent_rows = front_rest[0], parent_front[0]
    rows_here, pivot_order = pivot_rows.shape
    block_rows, child_order = rest_rows.shape
    window = parent_rows.shape[0]
    child_half = child_order // 2
    blocks = child_half // block_rows
    near = prows // 2
    leaf_index = lax.axis_index("leaf")
    side = leaf_index % 2
    partner = leaf_index + 1 - 2 * side

    def to_sibling(value):
        return lax.ppermute(value, "leaf", [(g, g ^ 1) for g in range(leaves)])

    def to_cols(value, apart, swap):
        pairs = [
            ((g * prows + r) * pcols + c, ((g ^ swap) * prows + r) * pcols + (c + apart) % pcols)
            for g in range(leaves)
            for r in range(prows)
            for c in range(pcols)
        ]
        return lax.ppermute(value, ("leaf",) + ROWS, pairs)

    def links_of(child):
        links = lax.dynamic_index_in_dim(relation, child, 0, keepdims=False)
        rows = lax.dynamic_slice_in_dim(links, position * block_rows, block_rows, 0)
        cols = lax.dynamic_slice_in_dim(links, side * child_half, child_half, 0)
        cols = cols.reshape(blocks, 1, 1, block_rows)
        first = side * blocks + jnp.arange(blocks, dtype=jnp.int32)
        return (
            (rows - position * window).reshape(1, 1, block_rows),
            cols - first.reshape(blocks, 1, 1, 1) * window,
        )

    own_row_links, own_col_links = links_of(leaf_index)
    other_row_links, other_col_links = links_of(partner)
    row_links = (own_row_links, other_row_links)
    col_links = (own_col_links, other_col_links)

    widths = panel_widths(pivot_order)
    starts = [sum(widths[:p]) for p in range(len(widths))]
    def along(value, step):
        return lax.ppermute(value, "prow", [(r, (r + step) % prows) for r in range(prows)])

    across_z = rows_here * pcols
    column_blocks = []
    spans = [(starts[0], starts[1]), (starts[1], starts[2]), (starts[2], pivot_order)]
    for n, (s, end) in enumerate(spans):
        mine = pivot_rows[:, s:end]
        if n == 0:
            mine = jnp.stack([mine] + [along(mine, step) for step in range(1, prows)])
        else:
            mine = lax.all_gather(mine, "prow", axis=0)[s // across_z:]
        column_blocks.append([mine] + [to_cols(mine, apart, 0) for apart in range(1, pcols)])

    def update(total, p, before_first, before_last):
        rounded, other, owns, others = panels[p]
        rows = spread_rows(rounded, other, row_links, window)
        for apart in range(pcols):
            places = jnp.arange(near, dtype=jnp.int32) * pcols + lax.rem(
                across - apart + pcols, pcols
            ).astype(jnp.int32)
            total = update_windows(
                total,
                rows,
                owns[apart],
                others[apart],
                places,
                col_links,
                before_last if apart == pcols - 1 else () if apart else before_first,
            )
        return total

    own_block = (position - side * blocks).astype(jnp.int32)
    done, panels, lines = [], [], []
    place = jnp.stack([lax.axis_index("prow"), across, side]).astype(jnp.int32)

    def pass_on(p, side_now):
        rounded, other, line = lines[p]
        kept = lax.dynamic_slice_in_dim(line, side_now * near, near, 0)
        sent = lax.dynamic_slice_in_dim(line, (1 - side_now) * near, near, 0)
        owns = [to_cols(kept, apart, 0) if apart else kept for apart in range(pcols)]
        others = [to_cols(sent, apart, 1) for apart in range(pcols)]
        panels.append((rounded, other, owns, others))
        return (kept, sent), tuple(owns[1:] + others)

    parts = []
    for p, (s, w) in enumerate(zip(starts, widths)):
        n = min(p, len(spans) - 1)
        if p == 0:
            waits = tuple(column_blocks[1]) + (column_blocks[2][0],)
        elif p == 1:
            start_total, leaving = add_rest(
                parent_rows,
                rest_rows,
                jnp.stack([side.astype(jnp.int32), own_block]),
                own_row_links,
                own_col_links,
                (done[0][0],),
                True,
            )
            waits = (start_total,)
        elif p == 3:
            total = add_rest(
                start_total,
                to_sibling(leaving),
                jnp.stack([jnp.zeros((), jnp.int32), own_block]),
                other_row_links,
                other_col_links,
                (),
                False,
            )
            total = update(total, 0, parts[1][0], ())
            waits = (total,)
        corner_at = (s // across_z - spans[n][0] // across_z, s - spans[n][0])
        pivot, lower, rounded, side_now = factor_panel(
            s, w, place, column_blocks[n], p == 0, corner_at, lower_rows, done, waits
        )
        done.append((pivot, lower))
        lines.append((rounded, to_sibling(rounded), lax.all_gather(rounded, "prow", axis=0)))
        if p:
            parts.append(pass_on(p - 1, side_now[0]))
    parts.append(pass_on(len(starts) - 1, side_now[0]))

    for p in range(1, len(starts)):
        total = update(total, p, parts[p][1] if p == 1 else (), ())

    factor_rows = jnp.concatenate(
        [
            lax.dynamic_slice_in_dim(
                jnp.concatenate([jnp.zeros((pivot_order - pivot.shape[0], w), f32), pivot], axis=0),
                position * rows_here,
                rows_here,
                0,
            )
            for s, w, (pivot, _) in zip(starts, widths, done)
        ],
        axis=1,
    )
    lower_out = jnp.concatenate([lower for _, lower in done], axis=1)
    return (factor_rows[None], lower_out[None], total[None])


def solution(mesh):
    whole = P("leaf", ROWS, None)
    return jax.shard_map(
        local,
        mesh=mesh,
        in_specs=(whole, whole, whole, whole, P()),
        out_specs=(whole, whole, whole),
        check_vma=False,
    )
```

```python
import math

import jax
import jax.numpy as jnp
from jax import lax
from jax.experimental import pallas as pl
from jax.experimental.pallas import tpu as pltpu
from jax.sharding import PartitionSpec as P

ROWS = ("prow", "pcol")
bf16 = jnp.bfloat16
f32 = jnp.float32
LANES = 128
SUBS = 8
GROUP = 32
TALL = 768
VMEM_LIMIT = 56 << 20


def panel_widths(order):
    narrow = order // 6
    return (narrow, 2 * narrow, 2 * narrow, narrow)


def split(x):
    top = x.astype(bf16)
    return top, (x - top.astype(f32)).astype(bf16)


def left_parts(x):
    top, low = split(x)
    return jnp.concatenate([top, top, low], axis=1)


def right_parts(x):
    top, low = split(x)
    return jnp.concatenate([top, low, top], axis=1)


def nt(a, b):
    return lax.dot_general(a, b, (((1,), (1,)), ((), ())), preferred_element_type=f32)


def nn(a, b):
    return jnp.dot(a, b, preferred_element_type=f32)


def spread_lane(x, lane):
    return jnp.broadcast_to(x[:, lane:lane + 1], (SUBS, LANES))


def spread_sub(x, sub):
    return jnp.broadcast_to(x[sub:sub + 1, :], (SUBS, LANES))


def factor_square(square):
    lane = lax.broadcasted_iota(jnp.int32, (SUBS, LANES), 1)
    sub = lax.broadcasted_iota(jnp.int32, (SUBS, LANES), 0)
    count = LANES // SUBS
    span = GROUP // SUBS
    state = [square[SUBS * r:SUBS * (r + 1), :] for r in range(count)]
    inverses = []
    for b in range(count):
        first = SUBS * b
        last = (b // span + 1) * span
        block = state[b]
        inside = (lane >= first) & (lane < first + SUBS)
        columns = [spread_lane(block, first + k) for k in range(SUBS)]
        d = [
            [spread_sub(columns[k], i) if k >= i else None for k in range(SUBS)]
            for i in range(SUBS)
        ]
        packed = jnp.where(inside, (lane - first == sub).astype(f32), block)
        rows = [spread_sub(packed, i) for i in range(SUBS)]
        follow = b + 1 < last
        if follow:
            ahead = state[b + 1]
            beside = [spread_lane(ahead, first + k) for k in range(SUBS)]
            ahead = jnp.where(inside, 0.0, ahead)
        scales, steps = [], []
        for i in range(SUBS):
            scale = lax.rsqrt(d[i][i])
            scales.append(scale)
            step = [d[i][k] * scale if k > i else None for k in range(SUBS)]
            steps.append(step)
            rows[i] = rows[i] * scale
            for k in range(i + 1, SUBS):
                for m in range(k, SUBS):
                    d[k][m] = d[k][m] - step[k] * step[m]
            for k in range(i + 1, SUBS):
                rows[k] = rows[k] - step[k] * rows[i]
            if follow:
                beside[i] = beside[i] * scale
                ahead = ahead - beside[i] * rows[i]
                for k in range(i + 1, SUBS):
                    beside[k] = beside[k] - step[k] * beside[i]
        whole = rows[0]
        for i in range(1, SUBS):
            whole = jnp.where(sub == i, rows[i], whole)
        inverses.append(whole)
        if follow:
            state[b + 1] = ahead
        if b + 2 < last:
            back = [None] * SUBS
            for i in reversed(range(SUBS)):
                total = rows[i]
                for k in range(i + 1, SUBS):
                    total = total - steps[i][k] * back[k]
                back[i] = total * scales[i]
            for r in range(b + 2, last):
                below = state[r]
                left = [spread_lane(below, first + k) for k in range(SUBS)]
                below = jnp.where(inside, 0.0, below)
                for k in range(SUBS):
                    below = below - left[k] * back[k]
                state[r] = below
        if b + 1 == last and last < count:
            start = GROUP * (b // span)
            solved = jnp.concatenate(
                [
                    jnp.where((lane >= SUBS * (g + 1)) & (lane < SUBS * last), 0.0, inverses[g])
                    for g in range(b + 1 - span, b + 1)
                ],
                axis=0,
            )
            after = jnp.concatenate(state[last:], axis=0)
            own = slice(start, start + GROUP)
            left = nt(left_parts(after[:, own]), right_parts(solved[:, own]))
            top, low = split(solved)
            change = nn(left_parts(left), jnp.concatenate([top, low, top], axis=0))
            for r in range(last, count):
                at = SUBS * (r - last)
                done = (lane >= start) & (lane < start + GROUP)
                state[r] = jnp.where(done, 0.0, state[r]) - change[at:at + SUBS, :]
    return jnp.concatenate(
        [jnp.where(lane < SUBS * (b + 1), inverses[b], 0.0) for b in range(count)], axis=0
    )


def largest_tile(rows):
    return next(t for t in (256, 128, 64, 32, 16, 8) if rows % t == 0)


def tall_tile(rows):
    return next(rows // n for n in range(1, rows) if rows % n == 0 and rows // n <= TALL)


def panel_kernel(first, base, bases, pcols, turned, corner_at, *refs):
    refs = list(refs)
    place, shares, refs = refs[0], refs[1:1 + pcols], refs[1 + pcols:]
    before = len(bases)
    earlier = [(refs[2 * q], refs[2 * q + 1]) for q in range(before)]
    refs = refs[2 * before:]
    waits = len(refs) - 5 - before
    lower_in = refs[0]
    pivot, lower, rounded, side, tops = refs[waits:waits + 5]
    crowns = refs[waits + 5:]
    side[0] = place[2]
    width = pivot.shape[1]
    count = width // LANES
    skip = first - base
    bottom = skip + width
    for q in range(before):
        for t in range(count):
            at = first - bases[q] + t * LANES
            crowns[q][t * LANES:(t + 1) * LANES, :] = right_parts(
                earlier[q][0][at:at + LANES, :]
            )
    low, left = corner_at
    prows, share_rows = shares[0].shape[:2]
    for apart in range(pcols):
        source = lax.rem(place[1] - apart + pcols, pcols)
        for r in range(prows - low):
            line = lax.rem(place[0] - r + prows, prows) if turned else r
            at = pl.multiple_of((line * pcols + source) * share_rows, 8)
            pivot[pl.ds(at, share_rows), :] = shares[apart][low + r, :, left:left + width]
    pltpu.sync_copy(lower_in.at[:, first:first + width], lower)

    def subtract(target, pasts, offsets):
        tile = tall_tile(target.shape[0])

        @pl.loop(0, target.shape[0] // tile)
        def _(t):
            at = pl.multiple_of(t * tile, tile)
            values = target[pl.ds(at, tile), :]
            for q in range(before):
                past = pasts[q][pl.ds(pl.multiple_of(offsets[q] + at, 8), tile), :]
                values = values - nt(left_parts(past), crowns[q][...])
            target[pl.ds(at, tile), :] = values

    if before:
        subtract(pivot, [past for past, _ in earlier], [base - b for b in bases])
        subtract(lower, [past for _, past in earlier], [0] * before)
    if skip:
        pivot[0:skip, :] = jnp.zeros((skip, width), f32)

    row = lax.broadcasted_iota(jnp.int32, (width, LANES), 0)
    lane = lax.broadcasted_iota(jnp.int32, (width, LANES), 1)

    @pl.loop(0, count)
    def _(k):
        here = pl.ds(pl.multiple_of(k * LANES, LANES), LANES)
        corner = pl.ds(pl.multiple_of(skip + k * LANES, LANES), LANES)
        solver = right_parts(factor_square(pivot[corner, here]))
        solved = nt(left_parts(pivot[skip:bottom, here]), solver)
        solved = jnp.where(row - k * LANES >= lane, solved, 0.0)
        pivot[skip:bottom, here] = solved
        solved = jnp.where(row >= (k + 1) * LANES, solved, 0.0)
        tops[...] = right_parts(solved)
        if count > 1:
            pivot[skip:bottom, LANES:] -= nt(left_parts(solved), tops[LANES:, :])

        def run(ref, start, rows):
            tile = tall_tile(rows)

            @pl.loop(0, rows // tile)
            def _(t):
                band = pl.ds(pl.multiple_of(start + t * tile, 8), tile)
                solved = nt(left_parts(ref[band, here]), solver)
                ref[band, here] = solved
                if count > 1:
                    ref[band, LANES:] -= nt(left_parts(solved), tops[LANES:, :])

        if pivot.shape[0] > bottom:
            run(pivot, bottom, pivot.shape[0] - bottom)
        run(lower, 0, lower.shape[0])

    tile = largest_tile(lower.shape[0])

    @pl.loop(0, lower.shape[0] // tile)
    def _(t):
        here = pl.ds(pl.multiple_of(t * tile, tile), tile)
        rounded[here, :] = lower[here, :].astype(bf16)


def factor_panel(first, width, place, shares, turned, corner_at, lower, earlier, after):
    prows, share_rows, _ = shares[0].shape
    rows = len(shares) * (prows - corner_at[0]) * share_rows
    order = lower.shape[1]
    base = order - rows
    flat = [past for pair in earlier for past in pair]
    in_vmem = pl.BlockSpec(memory_space=pltpu.VMEM)
    anywhere = pl.BlockSpec(memory_space=pl.ANY)
    bases = [order - past.shape[0] for past, _ in earlier]
    return pl.pallas_call(
        lambda *refs: panel_kernel(first, base, bases, len(shares), turned, corner_at, *refs),
        out_shape=(
            jax.ShapeDtypeStruct((rows, width), f32),
            jax.ShapeDtypeStruct((lower.shape[0], width), f32),
            jax.ShapeDtypeStruct((lower.shape[0], width), bf16),
            jax.ShapeDtypeStruct((1,), jnp.int32),
        ),
        in_specs=[pl.BlockSpec(memory_space=pltpu.SMEM)]
        + [in_vmem] * (len(shares) + len(flat))
        + [anywhere] * (1 + len(after)),
        out_specs=[in_vmem] * 3 + [pl.BlockSpec(memory_space=pltpu.SMEM)],
        scratch_shapes=[pltpu.VMEM((width, 3 * LANES), bf16)]
        + [pltpu.VMEM((width, 3 * past.shape[1]), bf16) for past, _ in earlier],
        compiler_params=pltpu.CompilerParams(vmem_limit_bytes=VMEM_LIMIT),
        cost_estimate=pl.CostEstimate(
            flops=width * 50000000,
            bytes_accessed=10 * width * (rows + lower.shape[0]),
            transcendentals=0,
        ),
    )(place, *shares, *flat, lower, *after)


def one_hot(links, window):
    places = lax.broadcasted_iota(jnp.int32, (window, links.shape[1]), 0)
    return (places == links).astype(bf16)


def rest_kernel(whole, half, values, *refs):
    out, table, placed = refs[-3:]
    if whole:
        out, leaving = refs[-4:-2]
        leaving[...] = refs[0][...]
        refs = refs[1:]
    row_links, col_links, parent = refs[:3]
    window = out.shape[0]
    rows = values.shape[0]

    @pl.when(pl.program_id(0) == 0)
    def _():
        spread = one_hot(row_links[0], window)
        table[:, :rows] = spread
        table[:, rows:] = spread

    tile = largest_tile(out.shape[1])
    count = col_links.shape[0]
    step = pl.program_id(0)
    mine = (half[1] >= step * count) & (half[1] < (step + 1) * count)

    def spread_of(part, at, depth):
        for i in range(count):
            spread = one_hot(col_links[i, 0], window)
            block, area = slice(i * rows, (i + 1) * rows), slice(i * window, (i + 1) * window)
            placed[at:at + rows, area] = nt(part[:, block], spread).astype(bf16)
        if depth:

            @pl.loop(0, out.shape[1] // tile)
            def _(t):
                here = pl.ds(pl.multiple_of(t * tile, tile), tile)
                out[:, here] = parent[:, here] + nn(table[:, :depth], placed[:depth, here])

    @pl.when(mine)
    def _():
        top, low = split(values[...])
        spread_of(top, 0, 0)
        spread_of(low, rows, 2 * rows)

    @pl.when(jnp.logical_not(mine))
    def _():
        spread_of(values[...].astype(bf16), 0, rows)


def add_rest(parent, values, half, row_links, col_links, after, whole):
    window = parent.shape[0]
    rows = values.shape[0]
    group = LANES // math.gcd(LANES, rows)
    steps = parent.shape[1] // window // group
    area = pl.BlockSpec((window, group * window), lambda w, half: (0, w))
    block = (rows, group * rows)
    total = jax.ShapeDtypeStruct(parent.shape, f32)
    crossing = [pl.BlockSpec(block, lambda w, half: (0, (1 - half[0]) * steps + w))]
    leaving = pl.BlockSpec(block, lambda w, half: (0, w))
    return pl.pallas_call(
        lambda *refs: rest_kernel(whole, *refs),
        out_shape=(total, jax.ShapeDtypeStruct((rows, values.shape[1] // 2), f32)) if whole else total,
        grid_spec=pltpu.PrefetchScalarGridSpec(
            num_scalar_prefetch=1,
            grid=(steps,),
            in_specs=[pl.BlockSpec(block, lambda w, half: (0, half[0] * steps + w))]
            + (crossing if whole else [])
            + [
                pl.BlockSpec((1, 1, rows), lambda w, half: (0, 0, 0)),
                pl.BlockSpec((group, 1, 1, rows), lambda w, half: (w, 0, 0, 0)),
                area,
            ]
            + [pl.BlockSpec(memory_space=pl.ANY)] * len(after),
            out_specs=(area, leaving) if whole else area,
            scratch_shapes=[
                pltpu.VMEM((window, 2 * rows), bf16),
                pltpu.VMEM((2 * rows, group * window), bf16),
            ],
        ),
        input_output_aliases={} if whole else {4: 0},
        compiler_params=pltpu.CompilerParams(vmem_limit_bytes=VMEM_LIMIT),
        cost_estimate=pl.CostEstimate(
            flops=4 * rows * parent.size + 4 * rows * rows * parent.shape[1],
            bytes_accessed=8 * parent.size + 4 * rows * rows * steps * group,
            transcendentals=0,
        ),
    )(
        half,
        *([values] * (2 if whole else 1)),
        row_links,
        col_links,
        parent,
        *after,
    )


def rows_kernel(own, other, own_links, other_links, out):
    window, width = out.shape[0], own.shape[1]
    for source, (values, links) in enumerate(((own, own_links), (other, other_links))):
        out[:, source * width:(source + 1) * width] = nn(
            one_hot(links[0], window), values[...]
        ).astype(bf16)


def spread_rows(own, other, row_links, window):
    return pl.pallas_call(
        rows_kernel,
        out_shape=jax.ShapeDtypeStruct((window, 2 * own.shape[1]), bf16),
        compiler_params=pltpu.CompilerParams(vmem_limit_bytes=VMEM_LIMIT),
        cost_estimate=pl.CostEstimate(
            flops=4 * window * own.size, bytes_accessed=12 * own.size, transcendentals=0
        ),
    )(own, other, *row_links)


def update_kernel(places, rows, own, other, own_links, other_links, total, *refs):
    out, cols = refs[-2:]
    window, width = cols.shape[0], own.shape[2]

    @pl.when(pl.program_id(1) == 0)
    def _():
        for source, (values, links) in enumerate(((own, own_links), (other, other_links))):
            cols[:, source * width:(source + 1) * width] = nn(
                one_hot(links[0, 0], window), values[0]
            ).astype(bf16)

    tile = out.shape[1]
    here = pl.ds(pl.multiple_of(pl.program_id(1) * tile, tile), tile)
    out[...] = total[...] - nt(rows[...], cols[here, :])


def update_windows(total, rows, own, other, places, col_links, after):
    window = total.shape[0]
    count, children, width = own.shape
    tile = largest_tile(window)
    block = pl.BlockSpec((1, children, width), lambda i, t, places: (i, 0, 0))
    link = pl.BlockSpec((1, 1, 1, children), lambda i, t, places: (places[i], 0, 0, 0))
    area = pl.BlockSpec(
        (window, tile), lambda i, t, places: (0, places[i] * (window // tile) + t)
    )
    return pl.pallas_call(
        update_kernel,
        out_shape=jax.ShapeDtypeStruct(total.shape, f32),
        grid_spec=pltpu.PrefetchScalarGridSpec(
            num_scalar_prefetch=1,
            grid=(count, window // tile),
            in_specs=[
                pl.BlockSpec((window, 2 * width), lambda i, t, places: (0, 0)),
                block,
                block,
                link,
                link,
                area,
            ]
            + [pl.BlockSpec(memory_space=pl.ANY)] * len(after),
            out_specs=area,
            scratch_shapes=[pltpu.VMEM((window, 2 * width), bf16)],
        ),
        input_output_aliases={6: 0},
        compiler_params=pltpu.CompilerParams(vmem_limit_bytes=VMEM_LIMIT),
        cost_estimate=pl.CostEstimate(
            flops=4 * count * window * width * (window + children),
            bytes_accessed=8 * count * window * window,
            transcendentals=0,
        ),
    )(places, rows, own, other, *col_links, total, *after)


def local(front_pivot, front_lower, front_rest, parent_front, relation):
    leaves, prows, pcols = (lax.axis_size(a) for a in ("leaf", "prow", "pcol"))
    position = lax.axis_index(ROWS)
    across = lax.axis_index("pcol")
    pivot_rows, lower_rows = front_pivot[0], front_lower[0]
    rest_rows, parent_rows = front_rest[0], parent_front[0]
    rows_here, pivot_order = pivot_rows.shape
    block_rows, child_order = rest_rows.shape
    window = parent_rows.shape[0]
    child_half = child_order // 2
    blocks = child_half // block_rows
    near = prows // 2
    leaf_index = lax.axis_index("leaf")
    side = leaf_index % 2
    partner = leaf_index + 1 - 2 * side

    def to_sibling(value):
        return lax.ppermute(value, "leaf", [(g, g ^ 1) for g in range(leaves)])

    def to_cols(value, apart, swap):
        pairs = [
            ((g * prows + r) * pcols + c, ((g ^ swap) * prows + r) * pcols + (c + apart) % pcols)
            for g in range(leaves)
            for r in range(prows)
            for c in range(pcols)
        ]
        return lax.ppermute(value, ("leaf",) + ROWS, pairs)

    def links_of(child):
        links = lax.dynamic_index_in_dim(relation, child, 0, keepdims=False)
        rows = lax.dynamic_slice_in_dim(links, position * block_rows, block_rows, 0)
        cols = lax.dynamic_slice_in_dim(links, side * child_half, child_half, 0)
        cols = cols.reshape(blocks, 1, 1, block_rows)
        first = side * blocks + jnp.arange(blocks, dtype=jnp.int32)
        return (
            (rows - position * window).reshape(1, 1, block_rows),
            cols - first.reshape(blocks, 1, 1, 1) * window,
        )

    own_row_links, own_col_links = links_of(leaf_index)
    other_row_links, other_col_links = links_of(partner)
    row_links = (own_row_links, other_row_links)
    col_links = (own_col_links, other_col_links)

    widths = panel_widths(pivot_order)
    starts = [sum(widths[:p]) for p in range(len(widths))]
    def along(value, step):
        return lax.ppermute(value, "prow", [(r, (r + step) % prows) for r in range(prows)])

    across_z = rows_here * pcols
    column_blocks = []
    spans = [(starts[0], starts[1]), (starts[1], starts[2]), (starts[2], pivot_order)]
    for n, (s, end) in enumerate(spans):
        mine = pivot_rows[:, s:end]
        if n == 0:
            mine = jnp.stack([mine] + [along(mine, step) for step in range(1, prows)])
        else:
            mine = lax.all_gather(mine, "prow", axis=0)[s // across_z:]
        column_blocks.append([mine] + [to_cols(mine, apart, 0) for apart in range(1, pcols)])

    def update(total, p, before_first, before_last):
        rounded, other, owns, others = panels[p]
        rows = spread_rows(rounded, other, row_links, window)
        for apart in range(pcols):
            places = jnp.arange(near, dtype=jnp.int32) * pcols + lax.rem(
                across - apart + pcols, pcols
            ).astype(jnp.int32)
            total = update_windows(
                total,
                rows,
                owns[apart],
                others[apart],
                places,
                col_links,
                before_last if apart == pcols - 1 else () if apart else before_first,
            )
        return total

    own_block = (position - side * blocks).astype(jnp.int32)
    done, panels, lines = [], [], []
    place = jnp.stack([lax.axis_index("prow"), across, side]).astype(jnp.int32)

    def pass_on(p, side_now):
        rounded, other, line = lines[p]
        kept = lax.dynamic_slice_in_dim(line, side_now * near, near, 0)
        sent = lax.dynamic_slice_in_dim(line, (1 - side_now) * near, near, 0)
        owns = [to_cols(kept, apart, 0) if apart else kept for apart in range(pcols)]
        others = [to_cols(sent, apart, 1) for apart in range(pcols)]
        panels.append((rounded, other, owns, others))
        return (kept, sent), tuple(owns[1:] + others)

    parts = []
    for p, (s, w) in enumerate(zip(starts, widths)):
        n = min(p, len(spans) - 1)
        if p == 0:
            start_total, leaving = add_rest(
                parent_rows,
                rest_rows,
                jnp.stack([side.astype(jnp.int32), own_block]),
                own_row_links,
                own_col_links,
                (column_blocks[0][-1], column_blocks[1][0]),
                True,
            )
            waits = (start_total,) + tuple(column_blocks[2])
        elif p == 3:
            total = add_rest(
                start_total,
                to_sibling(leaving),
                jnp.stack([jnp.zeros((), jnp.int32), own_block]),
                other_row_links,
                other_col_links,
                (),
                False,
            )
            total = update(total, 0, parts[1][0], ())
            waits = (total,)
        corner_at = (s // across_z - spans[n][0] // across_z, s - spans[n][0])
        pivot, lower, rounded, side_now = factor_panel(
            s, w, place, column_blocks[n], p == 0, corner_at, lower_rows, done, waits
        )
        done.append((pivot, lower))
        lines.append((rounded, to_sibling(rounded), lax.all_gather(rounded, "prow", axis=0)))
        if p:
            parts.append(pass_on(p - 1, side_now[0]))
    parts.append(pass_on(len(starts) - 1, side_now[0]))

    for p in range(1, len(starts)):
        total = update(total, p, parts[p][1] if p == 1 else (), ())

    factor_rows = jnp.concatenate(
        [
            lax.dynamic_slice_in_dim(
                jnp.concatenate([jnp.zeros((pivot_order - pivot.shape[0], w), f32), pivot], axis=0),
                position * rows_here,
                rows_here,
                0,
            )
            for s, w, (pivot, _) in zip(starts, widths, done)
        ],
        axis=1,
    )
    lower_out = jnp.concatenate([lower for _, lower in done], axis=1)
    return (factor_rows[None], lower_out[None], total[None])


def solution(mesh):
    whole = P("leaf", ROWS, None)
    return jax.shard_map(
        local,
        mesh=mesh,
        in_specs=(whole, whole, whole, whole, P()),
        out_specs=(whole, whole, whole),
        check_vma=False,
    )
```
